256 devices in a mesh: dp: 4 (over z_hi, core), context: 64 (over z_lo, x, y).
Axes of the slice: x: 4, y: 4, z: 8 (z_hi: 2, z_lo: 4; z = z_hi * 4 + z_lo), core: 2. Of those that a mesh axis runs over, the one named last changes fastest.
Arguments:
- grad_out: bfloat16 [4, 16384, 1024], P('dp', 'context'), may hold values from -6 to 6
- gate: bfloat16 [4, 16384, 1024], P('dp', 'context'), may hold values from -1.5 to 1.5
- key_in: bfloat16 [4, 16384, 1024], P('dp', 'context'), may hold values from -0.59765625 to 0.59765625
- value_in: bfloat16 [4, 16384, 1024], P('dp', 'context'), may hold values from -6 to 6
- filters: float32 [1024, 16384], P('context'), may hold values from -0.375 to 0.375
Outputs:
- grad_gate: bfloat16 [4, 16384, 1024], P('dp', 'context')
- grad_key: bfloat16 [4, 16384, 1024], P('dp', 'context')
- grad_value: bfloat16 [4, 16384, 1024], P('dp', 'context')
- grad_filter: float32 [1024, 16384], P(('context', 'dp'))
The draws below stay inside these ranges and needn't reach their ends.
All inputs are finite; a program needn't handle non-finite values.
Results may differ from the reference program's by a relative error of at most 0.015.
Values may be sent and summed in bfloat16 or wider, within the bound.
A program may use at most 128 MiB of HBM per device.

```python
import math
import jax
import jax.numpy as jnp
from jax import lax

C = 1024
LENGTH = 16384
SEQS = 4


def block_scale(stream_key, extent, shards, low, largest):
    def one(dim, parts):
        heights = jax.random.uniform(jax.random.fold_in(jax.random.fold_in(stream_key, 6), dim), (parts,), jnp.float32, low / len(shards), largest / len(shards))
        return jnp.repeat(jnp.exp(heights), extent[dim] // parts).reshape((-1,) + (1,) * (len(extent) - dim - 1))

    level = one(*shards[0])
    for cut in shards[1:]:
        level = level * one(*cut)
    return level


def bell_draw(key, shape, deviation, reach, cuts=(), kind=jnp.bfloat16):
    entries = deviation * jax.random.normal(key, shape, jnp.float32)
    if cuts:
        entries = entries * block_scale(key, shape, cuts, -0.22, 0.18)
    return jnp.clip(entries, -reach, reach).astype(kind)


def setup_inputs(seed: int = 0) -> dict:
    splits = jax.random.split(jax.random.key(seed), 6)
    return {
        "grad_out": bell_draw(splits[0], (SEQS, LENGTH, C), 1.0, 6.0, ((0, 4), (1, 64))),
        "gate": bell_draw(splits[1], (SEQS, LENGTH, C), 0.25, 1.5, ((0, 4), (1, 64))),
        "key_in": bell_draw(splits[2], (SEQS, LENGTH, C), 0.1, 0.59765625, ((0, 4), (1, 64))),
        "value_in": bell_draw(splits[3], (SEQS, LENGTH, C), 1.0, 6.0, ((0, 4), (1, 64))),
        "filters": bell_draw(splits[4], (C, LENGTH), (max(LENGTH // 64, 1)) ** -0.5, 0.375, ((0, 64),), jnp.float32),
    }


def channel_block(pieces):
    gated_block, keyval_block, filter_block = pieces
    length = gated_block.shape[-1]
    span_len = 2 * length
    gated_spec = jnp.fft.rfft(gated_block, n=span_len, axis=-1)
    keyval_spec = jnp.fft.rfft(keyval_block, n=span_len, axis=-1)
    filter_spec = jnp.fft.rfft(filter_block, n=span_len, axis=-1)
    conv = jnp.fft.irfft(filter_spec * keyval_spec, n=span_len, axis=-1)[:, :length]
    back = jnp.fft.irfft(gated_spec * jnp.conj(filter_spec), n=span_len, axis=-1)[:, :length]
    lagged = jnp.fft.irfft(gated_spec * jnp.conj(keyval_spec), n=span_len, axis=-1)[:, :length]
    return conv.astype(jnp.float32), back.astype(jnp.float32), lagged.astype(jnp.float32)


def reference(grad_out, gate, key_in, value_in, filters):
    keyvals = (key_in.astype(jnp.float32) * value_in.astype(jnp.float32)).astype(jnp.bfloat16)
    gated_grad = (grad_out.astype(jnp.float32) * gate.astype(jnp.float32)).astype(jnp.bfloat16)
    seq_count, length, channels = grad_out.shape
    block_size = math.gcd(channels, 128)
    blocks = channels // block_size
    filter_blocks = filters.reshape(blocks, block_size, length)
    grad_filter = jnp.zeros((channels, length), jnp.float32)
    gate_list, key_list, value_list = [], [], []
    for seq_index in range(seq_count):
        gated_cols = gated_grad[seq_index].astype(jnp.float32).T.reshape(blocks, block_size, length)
        keyval_cols = keyvals[seq_index].astype(jnp.float32).T.reshape(blocks, block_size, length)
        conv, back, lagged = lax.map(channel_block, (gated_cols, keyval_cols, filter_blocks))
        conv = conv.reshape(channels, length).T.astype(jnp.bfloat16).astype(jnp.float32)
        back = back.reshape(channels, length).T.astype(jnp.bfloat16).astype(jnp.float32)
        gate_list.append((grad_out[seq_index].astype(jnp.float32) * conv).astype(jnp.bfloat16))
        key_list.append((back * value_in[seq_index].astype(jnp.float32)).astype(jnp.bfloat16))
        value_list.append((back * key_in[seq_index].astype(jnp.float32)).astype(jnp.bfloat16))
        grad_filter = grad_filter + lagged.reshape(channels, length)
    return jnp.stack(gate_list), jnp.stack(key_list), jnp.stack(value_list), grad_filter
```

```python
import functools

import jax
import jax.numpy as jnp
import numpy as np
from jax import lax
from jax.experimental import pallas as pl
from jax.experimental.pallas import tpu as pltpu
from jax.sharding import PartitionSpec as P

MESH = pl.DeviceIdType.MESH
F32 = jnp.float32
BF16 = jnp.bfloat16

SPAN = 256
PARTS = 64
OWN = 16
HALF = 8
LENGTH = SPAN * PARTS


def tables():
    k1 = np.arange(PARTS)[:, None] + 0.25
    p = np.arange(PARTS)[None, :]
    angle = 2 * np.pi * k1 * p / PARTS
    first = np.concatenate([np.cos(angle), -np.sin(angle)], 0)
    zero = np.zeros_like(first)
    pair = np.block([[first, zero], [zero, first]])
    filt = np.concatenate([first, first], 1)
    last = np.concatenate([np.cos(angle).T, -np.sin(angle).T], 1) / LENGTH
    s = np.arange(SPAN)
    twist = 2 * np.pi * k1 * s[None, :] / LENGTH
    grid = 2 * np.pi * (s[:, None] * s[None, :] % SPAN) / SPAN
    cos, sin = np.cos(grid), np.sin(grid)
    forward = np.block([[cos, -sin], [sin, cos]])
    inverse = np.block([[cos, sin], [-sin, cos]])
    place = np.zeros((2, SPAN, 2 * SPAN))
    for h in range(2):
        for j in range(SPAN // OWN):
            for a in range(2):
                for c in range(HALF):
                    place[h, j * OWN + a * HALF + c, a * SPAN + j * OWN + h * HALF + c] = 1
    narrow = [np.asarray(t, dtype=jnp.bfloat16) for t in (pair, filt, last, forward, inverse)]
    return (
        *narrow,
        np.cos(twist).astype(np.float32),
        np.sin(twist).astype(np.float32),
        np.asarray(place, dtype=jnp.bfloat16),
        np.asarray(np.eye(SPAN), dtype=jnp.bfloat16),
    )


def dot(a, b):
    return jnp.dot(a, b, preferred_element_type=F32)


def dot_t(a, b):
    return lax.dot_general(a, b, (((1,), (1,)), ((), ())), preferred_element_type=F32)


def target(me, k):
    z, x, y = me // 16, (me // 4) % 4, me % 4
    return ((z + k % 4) % 4) * 16 + ((x + (k // 4) % 4) % 4) * 4 + (y + k // 16) % 4


def kernel(
    go, gt, ki, vi, flt, pair, filt, last, fwd, inv, tcos, tsin, place, eye,
    out_gate, out_key, out_value, out_filter,
    send_a, recv_a, send_b, recv_b, wide, back_wide, spec, lag, lag_out, lag_in, far_out, far_in,
    ss_a, rs_a, ss_b, rs_b, ss_l, rs_l, ss_f, rs_f,
):
    dp, me = lax.axis_index("dp"), lax.axis_index("context")
    z_hi, core = dp // 2, dp % 2
    other_core = z_hi * 2 + (1 - core)
    other_cube = (1 - z_hi) * 2 + core

    barrier = pltpu.get_barrier_semaphore()

    def greet(k, carry):
        pl.semaphore_signal(
            barrier, inc=1, device_id={"context": target(me, k)}, device_id_type=MESH
        )
        return carry

    lax.fori_loop(1, PARTS, greet, 0)
    pl.semaphore_signal(barrier, inc=1, device_id={"dp": other_core}, device_id_type=MESH)
    pl.semaphore_signal(barrier, inc=1, device_id={"dp": other_cube}, device_id_type=MESH)

    for b in range(4):
        cols = pl.ds(b * SPAN, SPAN)
        kv = (ki[:, cols].astype(F32) * vi[:, cols].astype(F32)).astype(BF16)
        gg = (go[:, cols].astype(F32) * gt[:, cols].astype(F32)).astype(BF16)
        both = jnp.concatenate([kv, gg], axis=1)
        for h in range(2):
            rows = dot_t(place[h], both).astype(BF16)
            send_a[h, pl.ds(b * 16, 16)] = rows.reshape(16, OWN, SPAN)

    pl.semaphore_wait(barrier, PARTS + 1)

    def scatter(src, dst, ssem, rsem, h):
        def one(k, carry):
            d = target(me, k)
            pltpu.make_async_remote_copy(
                src_ref=src.at[h, d],
                dst_ref=dst.at[h, me],
                send_sem=ssem.at[h],
                recv_sem=rsem.at[h],
                device_id={"context": d},
                device_id_type=MESH,
            ).start()
            return carry

        lax.fori_loop(1, PARTS, one, 0)
        dst[h, me] = src[h, me]

    def whole(src, dst, ssem, rsem, h):
        return pltpu.make_async_remote_copy(
            src_ref=src.at[h, pl.ds(0, PARTS - 1)],
            dst_ref=dst.at[h, pl.ds(0, PARTS - 1)],
            send_sem=ssem.at[h],
            recv_sem=rsem.at[h],
            device_id={"context": me},
            device_id_type=MESH,
        )

    order = (1 - z_hi, z_hi)
    for h in order:
        scatter(send_a, recv_a, ss_a, rs_a, h)

    def lay(p, carry):
        cols = pl.ds(pl.multiple_of(p * SPAN, SPAN), SPAN)
        for lanes in range(2):
            wide[lanes, pl.ds(pl.multiple_of(p * OWN, OWN), OWN), :] = flt[
                :, pl.ds(pl.multiple_of(p * SPAN + lanes * 128, 128), 128)
            ]
        return carry

    lax.fori_loop(0, PARTS, lay, 0)

    def column(ref, row):
        return jnp.concatenate(
            [ref[lanes, pl.ds(row, PARTS, stride=OWN), :] for lanes in range(2)], axis=1
        )

    def twist(mid):
        re, im = mid[:PARTS], mid[PARTS:]
        c, s = tcos[...], tsin[...]
        return jnp.concatenate([re * c + im * s, im * c - re * s], axis=1).astype(BF16)

    def filter_pair(i, carry):
        mids = []
        for n in range(2):
            x = column(wide, 2 * i + n)
            high = x.astype(BF16)
            low = (x - high.astype(F32)).astype(BF16)
            mids.append(twist(dot(filt[...], jnp.concatenate([high, low], axis=0))))
        full = dot(jnp.concatenate(mids, axis=0), fwd[...])
        spec[pl.ds(2 * i, 2)] = full.reshape(2, PARTS, 2 * SPAN)
        return carry

    lax.fori_loop(0, OWN // 2, filter_pair, 0)

    def convolve(h, slot):
        for lanes in range(2):
            wide[lanes] = (
                recv_a[h, :, :, pl.ds(lanes * 128, 128)].astype(F32).reshape(PARTS * OWN, 128)
            )

        def channel_pair(i, carry):
            mids = []
            for n in range(2):
                c = 2 * i + n
                x = jnp.concatenate([column(wide, c), column(wide, HALF + c)], axis=0)
                mid = dot(pair[...], x.astype(BF16))
                mids += [twist(mid[: 2 * PARTS]), twist(mid[2 * PARTS :])]
            full = dot(jnp.concatenate(mids, axis=0), fwd[...])
            prods = []
            for n in range(2):
                f = spec[h * HALF + 2 * i + n]
                fr, fi = f[:, :SPAN], f[:, SPAN:]
                kv = full[2 * n * PARTS : (2 * n + 1) * PARTS]
                gg = full[(2 * n + 1) * PARTS : (2 * n + 2) * PARTS]
                kr, kj = kv[:, :SPAN], kv[:, SPAN:]
                gr, gj = gg[:, :SPAN], gg[:, SPAN:]
                prods += [
                    jnp.concatenate([fr * kr - fi * kj, fr * kj + fi * kr], axis=1),
                    jnp.concatenate([gr * fr + gj * fi, gj * fr - gr * fi], axis=1),
                    jnp.concatenate([gr * kr + gj * kj, gj * kr - gr * kj], axis=1),
                ]
            mid = dot(jnp.concatenate([q.astype(BF16) for q in prods], axis=0), inv[...])
            co, si = tcos[...], tsin[...]
            for n in range(2):
                c = 2 * i + n
                for a in range(3):
                    top = (3 * n + a) * PARTS
                    re, im = mid[top : top + PARTS, :SPAN], mid[top : top + PARTS, SPAN:]
                    y = jnp.concatenate([re * co - im * si, im * co + re * si], axis=0)
                    line = dot(last[...], y.astype(BF16))
                    for lanes in range(2):
                        piece = line[:, lanes * 128 : (lanes + 1) * 128]
                        if a < 2:
                            back_wide[lanes, pl.ds(a * HALF + c, PARTS, stride=OWN), :] = piece
                        else:
                            lag[slot, c // 4, lanes, pl.ds(c % 4, PARTS, stride=4), :] = piece
            return carry

        lax.fori_loop(0, HALF // 2, channel_pair, 0)
        for lanes in range(2):
            send_b[h, :, :, pl.ds(lanes * 128, 128)] = (
                back_wide[lanes].astype(BF16).reshape(PARTS, OWN, 128)
            )

    def lag_swap(slot):
        return pltpu.make_async_remote_copy(
            src_ref=lag_out.at[slot],
            dst_ref=lag_in.at[slot],
            send_sem=ss_l.at[slot],
            recv_sem=rs_l.at[slot],
            device_id={"dp": other_core},
            device_id_type=MESH,
        )

    far = pltpu.make_async_remote_copy(
        src_ref=far_out,
        dst_ref=far_in,
        send_sem=ss_f.at[0],
        recv_sem=rs_f.at[0],
        device_id={"dp": other_cube},
        device_id_type=MESH,
    )

    for slot, h in enumerate(order):
        whole(send_a, recv_a, ss_a, rs_a, h).wait_recv()
        if slot == 1:
            lag_swap(0).wait_recv()
            far_out[...] = (lag[0, core] + lag_in[0].astype(F32)).astype(BF16)
            far.start()
        convolve(h, slot)
        scatter(send_b, recv_b, ss_b, rs_b, h)
        lag_out[slot] = lag[slot, 1 - core].astype(BF16)
        lag_swap(slot).start()

    lag_swap(1).wait_recv()
    far.wait_recv()
    for lanes in range(2):
        total = lag[1, core, lanes] + lag_in[1, lanes].astype(F32) + far_in[lanes].astype(F32)
        for p in range(PARTS):
            out_filter[:, pl.ds(p * SPAN + lanes * 128, 128)] = total[4 * p : 4 * p + 4]

    for h in order:
        whole(send_b, recv_b, ss_b, rs_b, h).wait_recv()
    for b in range(4):
        cols = pl.ds(b * SPAN, SPAN)
        groups = [recv_b[h, pl.ds(b * 16, 16)].astype(F32) for h in range(2)]
        turned = []
        for a in range(2):
            rows = jnp.concatenate([g[:, a * HALF : (a + 1) * HALF] for g in groups], axis=1)
            turned.append(dot_t(eye[...], rows.reshape(SPAN, SPAN).astype(BF16)))
        conv, back = turned
        out_gate[:, cols] = (go[:, cols].astype(F32) * conv).astype(BF16)
        out_key[:, cols] = (back * vi[:, cols].astype(F32)).astype(BF16)
        out_value[:, cols] = (back * ki[:, cols].astype(F32)).astype(BF16)

    for h in order:
        whole(send_a, recv_a, ss_a, rs_a, h).wait_send()
        whole(send_b, recv_b, ss_b, rs_b, h).wait_send()
    for slot in range(2):
        lag_swap(slot).wait_send()
    far.wait_send()


def on_device(grad_out, gate, key_in, value_in, filters):
    vmem = pl.BlockSpec(memory_space=pltpu.VMEM)
    consts = [jnp.asarray(t) for t in tables()]
    blocks = (2, PARTS, OWN, SPAN)
    dma = pltpu.SemaphoreType.DMA
    seq = jax.ShapeDtypeStruct((SPAN, 1024), BF16)
    grads = pl.pallas_call(
        kernel,
        out_shape=(seq, seq, seq, jax.ShapeDtypeStruct((4, LENGTH), F32)),
        in_specs=[vmem] * (5 + len(consts)),
        out_specs=(vmem,) * 4,
        scratch_shapes=[
            pltpu.VMEM(blocks, BF16),
            pltpu.VMEM(blocks, BF16),
            pltpu.VMEM(blocks, BF16),
            pltpu.VMEM(blocks, BF16),
            pltpu.VMEM((2, PARTS * OWN, 128), F32),
            pltpu.VMEM((2, PARTS * OWN, 128), F32),
            pltpu.VMEM((OWN, PARTS, 2 * SPAN), F32),
            pltpu.VMEM((2, 2, 2, PARTS * 4, 128), F32),
            pltpu.VMEM((2, 2, PARTS * 4, 128), BF16),
            pltpu.VMEM((2, 2, PARTS * 4, 128), BF16),
            pltpu.VMEM((2, PARTS * 4, 128), BF16),
            pltpu.VMEM((2, PARTS * 4, 128), BF16),
            dma((2,)), dma((2,)), dma((2,)), dma((2,)),
            dma((2,)), dma((2,)), dma((1,)), dma((1,)),
        ],
        name="hyena_backward",
        compiler_params=pltpu.CompilerParams(
            collective_id=0, has_side_effects=True, vmem_limit_bytes=48 * 2**20
        ),
    )(grad_out[0], gate[0], key_in[0], value_in[0], filters, *consts)
    return (grads[0][None], grads[1][None], grads[2][None], grads[3])


def solution(mesh):
    return jax.shard_map(
        on_device,
        mesh=mesh,
        in_specs=(
            P("dp", "context", None),
            P("dp", "context", None),
            P("dp", "context", None),
            P("dp", "context", None),
            P("context", None),
        ),
        out_specs=(
            P("dp", "context", None),
            P("dp", "context", None),
            P("dp", "context", None),
            P(("context", "dp"), None),
        ),
        check_vma=False,
    )
```

```python
import functools

import jax
import jax.numpy as jnp
import numpy as np
from jax import lax
from jax.experimental import pallas as pl
from jax.experimental.pallas import tpu as pltpu
from jax.sharding import PartitionSpec as P

MESH = pl.DeviceIdType.MESH
F32 = jnp.float32
BF16 = jnp.bfloat16

SPAN = 256
PARTS = 64
OWN = 16
HALF = 8
LENGTH = SPAN * PARTS
OPERANDS = 14


def tables():
    k1 = np.arange(PARTS)[:, None] + 0.25
    p = np.arange(PARTS)[None, :]
    angle = 2 * np.pi * k1 * p / PARTS
    first = np.concatenate([np.cos(angle), -np.sin(angle)], 0)
    zero = np.zeros_like(first)
    pair = np.block([[first, zero], [zero, first]])
    filt = np.concatenate([first, first], 1)
    last = np.concatenate([np.cos(angle).T, -np.sin(angle).T], 1) / LENGTH
    s = np.arange(SPAN)
    twist = 2 * np.pi * k1 * s[None, :] / LENGTH
    grid = 2 * np.pi * (s[:, None] * s[None, :] % SPAN) / SPAN
    cos, sin = np.cos(grid), np.sin(grid)
    forward = np.block([[cos, -sin], [sin, cos]])
    inverse = np.block([[cos, sin], [-sin, cos]])
    place = np.zeros((2, SPAN, 2 * SPAN))
    for h in range(2):
        for j in range(SPAN // OWN):
            for a in range(2):
                for c in range(HALF):
                    place[h, j * OWN + a * HALF + c, a * SPAN + j * OWN + h * HALF + c] = 1
    eye = np.eye(SPAN)
    return place, filt, np.cos(twist), np.sin(twist), forward, pair, inverse, last, eye


def dot(a, b):
    return jnp.dot(a, b, preferred_element_type=F32)


def dot_t(a, b):
    return lax.dot_general(a, b, (((1,), (1,)), ((), ())), preferred_element_type=F32)


def target(me, plane, k):
    x, y = (me // 4) % 4, me % 4
    return plane * 16 + ((x + k // 4) % 4) * 4 + (y + k % 4) % 4


def kernel(*refs):
    given, refs = refs[:OPERANDS], refs[OPERANDS:]
    results, refs = refs[:3], refs[3:]
    held, loaded, refs = refs[:OPERANDS], refs[OPERANDS], refs[OPERANDS + 1 :]
    loads = [
        pltpu.make_async_copy(src, dst, loaded.at[n])
        for n, (src, dst) in enumerate(zip(given, held))
    ]
    for load in loads:
        load.start()
    body(loads, *held, *results, *refs)


def body(
    loads,
    gt, ki, vi, go, place, flt, filt, tcos, tsin, fwd, pair, inv, last, eye,
    out_conv, out_back, out_filter,
    both, send_a, recv_a, send_b, recv_b, wide, back_wide, spec, lag, lag_out, lag_in, far_out, far_in,
    ss_a, rs_a, ss_b, rs_b, ss_l, rs_l, ss_f, rs_f,
):
    dp, me = lax.axis_index("dp"), lax.axis_index("context")
    z_hi, core = dp // 2, dp % 2
    other_core = z_hi * 2 + (1 - core)
    other_cube = (1 - z_hi) * 2 + core

    barrier = pltpu.get_barrier_semaphore()

    z = me // 16
    half, odd = z // 2, z % 2
    across, behind = (1 - half) * 2 + odd, (1 - half) * 2 + (1 - odd)
    beside = half * 2 + (1 - odd)
    planes = (across, behind, beside, z)

    for plane in planes:

        def greet(k, carry, plane=plane):
            pl.semaphore_signal(
                barrier, inc=1, device_id={"context": target(me, plane, k)}, device_id_type=MESH
            )
            return carry

        lax.fori_loop(1 if plane is z else 0, 16, greet, 0)
    pl.semaphore_signal(barrier, inc=1, device_id={"dp": other_core}, device_id_type=MESH)
    pl.semaphore_signal(barrier, inc=1, device_id={"dp": other_cube}, device_id_type=MESH)

    for load in loads[:5]:
        load.wait()
    order = (1 - z_hi, z_hi)

    def rows_of(h, plane):
        rows = dot_t(place[h], both[plane]).astype(BF16)
        send_a[h, pl.ds(plane * 16, 16)] = rows.reshape(16, OWN, SPAN)

    def send(src, dst, ssem, rsem, h, plane, k):
        d = target(me, plane, k)
        pltpu.make_async_remote_copy(
            src_ref=src.at[h, d],
            dst_ref=dst.at[h, me],
            send_sem=ssem.at[h],
            recv_sem=rsem.at[h],
            device_id={"context": d},
            device_id_type=MESH,
        ).start()

    def send_planes(src, dst, ssem, rsem, jobs):
        def one(k, carry):
            for h, plane in jobs:
                send(src, dst, ssem, rsem, h, plane, k)
            return carry

        lax.fori_loop(1, 16, one, 0)
        for h, plane in jobs:
            if plane is z:
                dst[h, me] = src[h, me]
            else:
                send(src, dst, ssem, rsem, h, plane, 0)

    first, second = order
    for n, plane in enumerate(planes):
        cols = pl.ds(pl.multiple_of(plane * SPAN, SPAN), SPAN)
        kv = (ki[:, cols].astype(F32) * vi[:, cols].astype(F32)).astype(BF16)
        gg = (go[:, cols].astype(F32) * gt[:, cols].astype(F32)).astype(BF16)
        both[plane] = jnp.concatenate([kv, gg], axis=1)
        rows_of(first, plane)
        if n == 0:
            pl.semaphore_wait(barrier, PARTS + 1)
        if n < 2:
            send_planes(send_a, recv_a, ss_a, rs_a, [(first, plane)])
    rows_of(second, across)
    rows_of(second, behind)
    send_planes(
        send_a, recv_a, ss_a, rs_a,
        [(first, beside), (second, across), (first, z), (second, behind)],
    )
    rows_of(second, beside)
    rows_of(second, z)
    send_planes(send_a, recv_a, ss_a, rs_a, [(second, beside), (second, z)])

    def whole(src, dst, ssem, rsem, h):
        return pltpu.make_async_remote_copy(
            src_ref=src.at[h, pl.ds(0, PARTS - 1)],
            dst_ref=dst.at[h, pl.ds(0, PARTS - 1)],
            send_sem=ssem.at[h],
            recv_sem=rsem.at[h],
            device_id={"context": me},
            device_id_type=MESH,
        )

    for load in loads[5:]:
        load.wait()

    def lay(p, carry):
        cols = pl.ds(pl.multiple_of(p * SPAN, SPAN), SPAN)
        for lanes in range(2):
            wide[lanes, pl.ds(pl.multiple_of(p * OWN, OWN), OWN), :] = flt[
                :, pl.ds(pl.multiple_of(p * SPAN + lanes * 128, 128), 128)
            ]
        return carry

    lax.fori_loop(0, PARTS, lay, 0)

    def column(ref, row):
        return jnp.concatenate(
            [ref[lanes, pl.ds(row, PARTS, stride=OWN), :] for lanes in range(2)], axis=1
        )

    def twist(mid):
        re, im = mid[:PARTS], mid[PARTS:]
        c, s = tcos[...], tsin[...]
        return jnp.concatenate([re * c + im * s, im * c - re * s], axis=1).astype(BF16)

    def filter_pair(i, carry):
        mids = []
        for n in range(2):
            x = column(wide, 2 * i + n)
            high = x.astype(BF16)
            low = (x - high.astype(F32)).astype(BF16)
            mids.append(twist(dot(filt[...], jnp.concatenate([high, low], axis=0))))
        full = dot(jnp.concatenate(mids, axis=0), fwd[...])
        spec[pl.ds(2 * i, 2)] = full.reshape(2, PARTS, 2 * SPAN)
        return carry

    lax.fori_loop(0, OWN // 2, filter_pair, 0)

    def convolve(h, slot):
        for lanes in range(2):
            wide[lanes] = (
                recv_a[h, :, :, pl.ds(lanes * 128, 128)].astype(F32).reshape(PARTS * OWN, 128)
            )

        def channel_pair(i, carry):
            mids = []
            for n in range(2):
                c = 2 * i + n
                x = jnp.concatenate([column(wide, c), column(wide, HALF + c)], axis=0)
                mid = dot(pair[...], x.astype(BF16))
                mids += [twist(mid[: 2 * PARTS]), twist(mid[2 * PARTS :])]
            full = dot(jnp.concatenate(mids, axis=0), fwd[...])
            prods = []
            for n in range(2):
                f = spec[h * HALF + 2 * i + n]
                fr, fi = f[:, :SPAN], f[:, SPAN:]
                kv = full[2 * n * PARTS : (2 * n + 1) * PARTS]
                gg = full[(2 * n + 1) * PARTS : (2 * n + 2) * PARTS]
                kr, kj = kv[:, :SPAN], kv[:, SPAN:]
                gr, gj = gg[:, :SPAN], gg[:, SPAN:]
                prods += [
                    jnp.concatenate([fr * kr - fi * kj, fr * kj + fi * kr], axis=1),
                    jnp.concatenate([gr * fr + gj * fi, gj * fr - gr * fi], axis=1),
                    jnp.concatenate([gr * kr + gj * kj, gj * kr - gr * kj], axis=1),
                ]
            mid = dot(jnp.concatenate([q.astype(BF16) for q in prods], axis=0), inv[...])
            co, si = tcos[...], tsin[...]
            for n in range(2):
                c = 2 * i + n
                for a in range(3):
                    top = (3 * n + a) * PARTS
                    re, im = mid[top : top + PARTS, :SPAN], mid[top : top + PARTS, SPAN:]
                    y = jnp.concatenate([re * co - im * si, im * co + re * si], axis=0)
                    line = dot(last[...], y.astype(BF16))
                    for lanes in range(2):
                        piece = line[:, lanes * 128 : (lanes + 1) * 128]
                        if a < 2:
                            back_wide[lanes, pl.ds(a * HALF + c, PARTS, stride=OWN), :] = piece
                        else:
                            lag[slot, c // 4, lanes, pl.ds(c % 4, PARTS, stride=4), :] = piece
            return carry

        lax.fori_loop(0, HALF // 2, channel_pair, 0)
        for lanes in range(2):
            send_b[h, :, :, pl.ds(lanes * 128, 128)] = (
                back_wide[lanes].astype(BF16).reshape(PARTS, OWN, 128)
            )

    def lag_swap(slot):
        return pltpu.make_async_remote_copy(
            src_ref=lag_out.at[slot],
            dst_ref=lag_in.at[slot],
            send_sem=ss_l.at[slot],
            recv_sem=rs_l.at[slot],
            device_id={"dp": other_core},
            device_id_type=MESH,
        )

    far = pltpu.make_async_remote_copy(
        src_ref=far_out,
        dst_ref=far_in,
        send_sem=ss_f.at[0],
        recv_sem=rs_f.at[0],
        device_id={"dp": other_cube},
        device_id_type=MESH,
    )

    for slot, h in enumerate(order):
        whole(send_a, recv_a, ss_a, rs_a, h).wait_recv()
        if slot == 1:
            lag_swap(0).wait_recv()
            far_out[...] = (lag[0, core] + lag_in[0].astype(F32)).astype(BF16)
            far.start()
        convolve(h, slot)
        send_planes(send_b, recv_b, ss_b, rs_b, [(h, across), (h, behind)])
        send_planes(send_b, recv_b, ss_b, rs_b, [(h, beside), (h, z)])
        lag_out[slot] = lag[slot, 1 - core].astype(BF16)
        lag_swap(slot).start()

    lag_swap(1).wait_recv()
    far.wait_recv()
    for lanes in range(2):
        total = lag[1, core, lanes] + lag_in[1, lanes].astype(F32) + far_in[lanes].astype(F32)
        for p in range(PARTS):
            out_filter[:, pl.ds(p * SPAN + lanes * 128, 128)] = total[4 * p : 4 * p + 4]

    for h in order:
        whole(send_b, recv_b, ss_b, rs_b, h).wait_recv()
    for b in range(4):
        cols = pl.ds(b * SPAN, SPAN)
        groups = [recv_b[h, pl.ds(b * 16, 16)].astype(F32) for h in range(2)]
        turned = []
        for a in range(2):
            rows = jnp.concatenate([g[:, a * HALF : (a + 1) * HALF] for g in groups], axis=1)
            turned.append(dot_t(eye[...], rows.reshape(SPAN, SPAN).astype(BF16)))
        out_conv[:, cols] = turned[0].astype(BF16)
        out_back[:, cols] = turned[1].astype(BF16)

    for h in order:
        whole(send_a, recv_a, ss_a, rs_a, h).wait_send()
        whole(send_b, recv_b, ss_b, rs_b, h).wait_send()
    for slot in range(2):
        lag_swap(slot).wait_send()
    far.wait_send()


def on_device(grad_out, gate, key_in, value_in, filters):
    vmem = pl.BlockSpec(memory_space=pltpu.VMEM)
    consts = [
        jnp.asarray(t.astype(np.float32) if n in (2, 3) else np.asarray(t, dtype=jnp.bfloat16))
        for n, t in enumerate(tables())
    ]
    place, *rest = consts
    operands = (gate[0], key_in[0], value_in[0], grad_out[0], place, filters, *rest)
    blocks = (2, PARTS, OWN, SPAN)
    dma = pltpu.SemaphoreType.DMA
    seq = jax.ShapeDtypeStruct((SPAN, 1024), BF16)
    conv, back, grad_filter = pl.pallas_call(
        kernel,
        out_shape=(seq, seq, jax.ShapeDtypeStruct((4, LENGTH), F32)),
        in_specs=[pl.BlockSpec(memory_space=pltpu.HBM)] * OPERANDS,
        out_specs=(vmem,) * 3,
        scratch_shapes=[
            *[pltpu.VMEM(x.shape, x.dtype) for x in operands],
            dma((OPERANDS,)),
            pltpu.VMEM((4, SPAN, 2 * SPAN), BF16),
            pltpu.VMEM(blocks, BF16),
            pltpu.VMEM(blocks, BF16),
            pltpu.VMEM(blocks, BF16),
            pltpu.VMEM(blocks, BF16),
            pltpu.VMEM((2, PARTS * OWN, 128), F32),
            pltpu.VMEM((2, PARTS * OWN, 128), F32),
            pltpu.VMEM((OWN, PARTS, 2 * SPAN), F32),
            pltpu.VMEM((2, 2, 2, PARTS * 4, 128), F32),
            pltpu.VMEM((2, 2, PARTS * 4, 128), BF16),
            pltpu.VMEM((2, 2, PARTS * 4, 128), BF16),
            pltpu.VMEM((2, PARTS * 4, 128), BF16),
            pltpu.VMEM((2, PARTS * 4, 128), BF16),
            dma((2,)), dma((2,)), dma((2,)), dma((2,)),
            dma((2,)), dma((2,)), dma((1,)), dma((1,)),
        ],
        name="hyena_backward",
        compiler_params=pltpu.CompilerParams(
            collective_id=0, has_side_effects=True, vmem_limit_bytes=63 * 2**20
        ),
    )(*operands)
    wide = back.astype(F32)
    grad_gate = (grad_out[0].astype(F32) * conv.astype(F32)).astype(BF16)
    grad_key = (wide * value_in[0].astype(F32)).astype(BF16)
    grad_value = (wide * key_in[0].astype(F32)).astype(BF16)
    return (grad_gate[None], grad_key[None], grad_value[None], grad_filter)


def solution(mesh):
    return jax.shard_map(
        on_device,
        mesh=mesh,
        in_specs=(
            P("dp", "context", None),
            P("dp", "context", None),
            P("dp", "context", None),
            P("dp", "context", None),
            P("context", None),
        ),
        out_specs=(
            P("dp", "context", None),
            P("dp", "context", None),
            P("dp", "context", None),
            P(("context", "dp"), None),
        ),
        check_vma=False,
    )
```

```python
import functools

import jax
import jax.numpy as jnp
import numpy as np
from jax import lax
from jax.experimental import pallas as pl
from jax.experimental.pallas import tpu as pltpu
from jax.sharding import PartitionSpec as P

MESH = pl.DeviceIdType.MESH
F32 = jnp.float32
BF16 = jnp.bfloat16

SPAN = 256
PARTS = 64
OWN = 16
HALF = 8
LENGTH = SPAN * PARTS
SIDE = PARTS // 2
OPERANDS = 18


def tables():
    k1 = np.arange(PARTS)[:, None] + 0.25
    p = np.arange(PARTS)[None, :]
    angle = 2 * np.pi * k1 * p / PARTS
    first = np.concatenate([np.cos(angle), -np.sin(angle)], 0)
    zero = np.zeros_like(first)
    pair = np.block([[first, zero], [zero, first]])
    filt = np.concatenate([first, first], 1)
    last = np.concatenate([np.cos(angle).T, -np.sin(angle).T], 1) / LENGTH
    s = np.arange(SPAN)
    twist = 2 * np.pi * k1 * s[None, :] / LENGTH
    grid = 2 * np.pi * (s[:, None] * s[None, :] % SPAN) / SPAN
    cos, sin = np.cos(grid), np.sin(grid)
    forward = np.block([[cos, -sin], [sin, cos]])
    inverse = np.block([[cos, sin], [-sin, cos]])
    place = np.zeros((2, SPAN, 2 * SPAN))
    for h in range(2):
        for j in range(SPAN // OWN):
            for a in range(2):
                for c in range(HALF):
                    place[h, j * OWN + a * HALF + c, a * SPAN + j * OWN + h * HALF + c] = 1
    eye = np.eye(SPAN)
    k1 = np.arange(SIDE)[:, None] + 0.25
    angle = 2 * np.pi * k1 * np.arange(SIDE)[None, :] / SIDE
    first = np.concatenate([np.cos(angle), -np.sin(angle)], 0)
    near = np.block([[first, np.zeros_like(first)], [np.zeros_like(first), first]])
    final = np.concatenate([np.cos(angle).T, -np.sin(angle).T], 1) * 2 / LENGTH
    near_last = np.block([[final, np.zeros_like(final)], [np.zeros_like(final), final]])
    near_twist = 2 * np.pi * k1 * s[None, :] * 2 / LENGTH
    return (
        np.cos(twist), np.sin(twist), np.cos(near_twist), np.sin(near_twist),
        place, eye, filt, forward, near, pair, inverse, last, near_last,
    )


def dot(a, b):
    return jnp.dot(a, b, preferred_element_type=F32)


def dot_t(a, b):
    return lax.dot_general(a, b, (((1,), (1,)), ((), ())), preferred_element_type=F32)


def target(me, plane, k):
    x, y = (me // 4) % 4, me % 4
    return plane * 16 + ((x + k // 4) % 4) * 4 + (y + k % 4) % 4


def kernel(*refs):
    given, refs = refs[:OPERANDS], refs[OPERANDS:]
    results, refs = refs[:3], refs[3:]
    held, loaded, refs = refs[:OPERANDS], refs[OPERANDS], refs[OPERANDS + 1 :]
    loads = [
        pltpu.make_async_copy(src, dst, loaded.at[n])
        for n, (src, dst) in enumerate(zip(given, held))
    ]
    for load in loads:
        load.start()
    body(loads, *held, *results, *refs)


def body(
    loads,
    gt, ki, vi, go, place, eye, flt, tcos, tsin, near_cos, near_sin,
    filt, fwd, near, pair, inv, last, near_last,
    out_conv, out_back, out_filter,
    both, send_a, recv_a, send_b, recv_b, send_c, recv_c, work_a, work_in, work_b, work_back,
    taps, near_taps, wide, back_wide, spec, near_spec, lag, lag_out, lag_in, far_out, far_in,
    ss_a, rs_a, ss_b, rs_b, ss_c, rs_c, ss_w, rs_w, ss_t, rs_t, ss_l, rs_l, ss_f, rs_f,
):
    dp, me = lax.axis_index("dp"), lax.axis_index("context")
    z_hi, core = dp // 2, dp % 2
    other_core = z_hi * 2 + (1 - core)
    other_cube = (1 - z_hi) * 2 + core

    barrier = pltpu.get_barrier_semaphore()

    z = me // 16
    half, odd = z // 2, z % 2
    across, behind = (1 - half) * 2 + odd, (1 - half) * 2 + (1 - odd)
    beside = half * 2 + (1 - odd)
    planes = (across, behind, beside, z)

    for plane in planes:

        def greet(k, carry, plane=plane):
            pl.semaphore_signal(
                barrier, inc=1, device_id={"context": target(me, plane, k)}, device_id_type=MESH
            )
            return carry

        lax.fori_loop(1 if plane is z else 0, 16, greet, 0)
    pl.semaphore_signal(barrier, inc=1, device_id={"dp": other_core}, device_id_type=MESH)
    pl.semaphore_signal(barrier, inc=1, device_id={"dp": other_cube}, device_id_type=MESH)
    twin = {"dp": other_cube, "context": (me + SIDE) % PARTS}
    pl.semaphore_signal(barrier, inc=1, device_id=twin, device_id_type=MESH)

    for load in loads[:7]:
        load.wait()
    order = (1 - z_hi, z_hi)

    def rows_of(h, plane):
        rows = dot_t(place[h], both[plane]).astype(BF16)
        send_a[h, pl.ds(plane * 16, 16)] = rows.reshape(16, OWN, SPAN)

    mine = me % SIDE

    def forward_block(h):
        return lambda d: (send_a.at[h, d], recv_a.at[h, me], ss_a.at[h], rs_a.at[h])

    def work_block(d):
        return work_a.at[d % SIDE], work_in.at[mine], ss_w.at[0], rs_w.at[0]

    def return_block(h):
        return lambda d: (send_b.at[h, d % SIDE], recv_b.at[h, mine], ss_b.at[h], rs_b.at[h])

    def far_block(h):
        return lambda d: (send_c.at[h, d % SIDE], recv_c.at[h, mine], ss_c.at[h], rs_c.at[h])

    def work_result(d):
        return work_b.at[d % SIDE], work_back.at[mine], ss_w.at[1], rs_w.at[1]

    def send(block, plane, k):
        d = target(me, plane, k)
        src, dst, ssem, rsem = block(d)
        pltpu.make_async_remote_copy(
            src_ref=src,
            dst_ref=dst,
            send_sem=ssem,
            recv_sem=rsem,
            device_id={"context": d},
            device_id_type=MESH,
        ).start()

    def send_planes(jobs):
        def one(k, carry):
            for block, plane in jobs:
                send(block, plane, k)
            return carry

        lax.fori_loop(1, 16, one, 0)
        for block, plane in jobs:
            if plane is z:
                src, dst, _, _ = block(me)
                dst[...] = src[...]
            else:
                send(block, plane, 0)

    def tap_copy(step):
        here = near_taps.at[core]
        return pltpu.make_async_remote_copy(
            src_ref=taps if step == 0 else here,
            dst_ref=here,
            send_sem=ss_t.at[step],
            recv_sem=rs_t.at[step],
            device_id=twin if step == 0 else {"dp": other_core},
            device_id_type=MESH,
        )

    first, second = order
    for n, plane in enumerate(planes):
        cols = pl.ds(pl.multiple_of(plane * SPAN, SPAN), SPAN)
        kv = (ki[:, cols].astype(F32) * vi[:, cols].astype(F32)).astype(BF16)
        gg = (go[:, cols].astype(F32) * gt[:, cols].astype(F32)).astype(BF16)
        both[plane] = jnp.concatenate([kv, gg], axis=1)
        rows_of(first, plane)
        if n == 0:
            taps[...] = flt[
                :, pl.ds(pl.multiple_of(core * (LENGTH // 4), LENGTH // 4), LENGTH // 4)
            ].astype(BF16)
            pl.semaphore_wait(barrier, PARTS + 2)
            tap_copy(0).start()
            send_planes([(forward_block(first), plane)])
    send_planes([(forward_block(first), p) for p in (beside, behind, z)])
    rows_of(second, across)
    rows_of(second, behind)
    for n in range(2):
        one_array = both[(1 - half) * 2 + n, :, pl.ds(pl.multiple_of(half * SPAN, SPAN), SPAN)]
        work_a[pl.ds(n * 16, 16)] = dot_t(eye[...], one_array).astype(BF16).reshape(16, OWN, SPAN)
    send_planes(
        [
            (forward_block(second), across), (work_block, beside),
            (forward_block(second), behind), (work_block, z),
        ]
    )
    rows_of(second, beside)
    rows_of(second, z)
    send_planes([(forward_block(second), beside), (forward_block(second), z)])

    def whole(src, dst, count, ssem, rsem):
        return pltpu.make_async_remote_copy(
            src_ref=src.at[pl.ds(0, count)],
            dst_ref=dst.at[pl.ds(0, count)],
            send_sem=ssem,
            recv_sem=rsem,
            device_id={"context": me},
            device_id_type=MESH,
        )

    def forward_whole(h):
        return whole(send_a.at[h], recv_a.at[h], PARTS - 1, ss_a.at[h], rs_a.at[h])

    def return_whole(h):
        return whole(send_b.at[h], recv_b.at[h], SIDE - 1, ss_b.at[h], rs_b.at[h])

    def far_whole(h):
        return whole(send_c.at[h], recv_c.at[h], SIDE, ss_c.at[h], rs_c.at[h])

    work_whole = whole(work_a, work_in, SIDE - 1, ss_w.at[0], rs_w.at[0])
    result_whole = whole(work_b, work_back, SIDE - 1, ss_w.at[1], rs_w.at[1])

    for load in loads[7:]:
        load.wait()

    def lay(p, carry):
        cols = pl.ds(pl.multiple_of(p * SPAN, SPAN), SPAN)
        for lanes in range(2):
            wide[lanes, pl.ds(pl.multiple_of(p * OWN, OWN), OWN), :] = flt[
                :, pl.ds(pl.multiple_of(p * SPAN + lanes * 128, 128), 128)
            ]
        return carry

    lax.fori_loop(0, PARTS, lay, 0)

    def column(ref, row, parts=PARTS):
        return jnp.concatenate(
            [ref[lanes, pl.ds(row, parts, stride=OWN), :] for lanes in range(2)], axis=1
        )

    def twist(mid, cos=tcos, sin=tsin):
        parts = cos.shape[0]
        re, im = mid[:parts], mid[parts:]
        c, s = cos[...], sin[...]
        return jnp.concatenate([re * c + im * s, im * c - re * s], axis=1).astype(BF16)

    def filter_pair(i, carry):
        mids = []
        for n in range(2):
            x = column(wide, 2 * i + n)
            high = x.astype(BF16)
            low = (x - high.astype(F32)).astype(BF16)
            mids.append(twist(dot(filt[...], jnp.concatenate([high, low], axis=0))))
        full = dot(jnp.concatenate(mids, axis=0), fwd[...])
        spec[pl.ds(2 * i, 2)] = full.reshape(2, PARTS, 2 * SPAN)
        return carry

    lax.fori_loop(0, OWN // 2, filter_pair, 0)

    def near_rows(i):
        mids = []
        for n in range(2):
            x = [column(wide, 4 * i + 2 * n + m, SIDE) for m in range(2)]
            mid = dot(near[...], jnp.concatenate(x, axis=0).astype(BF16))
            for m in range(2):
                mids.append(twist(mid[2 * m * SIDE : 2 * (m + 1) * SIDE], near_cos, near_sin))
        return dot(jnp.concatenate(mids, axis=0), fwd[...])

    tap_copy(0).wait_recv()
    tap_copy(1).start()
    tap_copy(1).wait_recv()
    for q in range(2):
        for p in range(SIDE // 2):
            for lanes in range(2):
                wide[lanes, pl.ds((q * SIDE // 2 + p) * OWN, OWN), :] = near_taps[
                    q, :, pl.ds(p * SPAN + lanes * 128, 128)
                ].astype(F32)

    def near_filters(i, carry):
        full = near_rows(i)
        im = jnp.where(half == 0, full[:, SPAN:], -full[:, SPAN:])
        full = jnp.concatenate([full[:, :SPAN], im], axis=1)
        near_spec[pl.ds(4 * i, 4)] = full.reshape(4, SIDE, 2 * SPAN)
        return carry

    lax.fori_loop(0, OWN // 4, near_filters, 0)

    def work():
        for lanes in range(2):
            wide[lanes, pl.ds(0, SIDE * OWN)] = (
                work_in[:, :, pl.ds(lanes * 128, 128)].astype(F32).reshape(SIDE * OWN, 128)
            )

        def four(i, carry):
            x = near_rows(i)
            f = near_spec[pl.ds(4 * i, 4)].reshape(4 * SIDE, 2 * SPAN)
            fr, fi = f[:, :SPAN], f[:, SPAN:]
            xr, xi = x[:, :SPAN], x[:, SPAN:]
            prod = jnp.concatenate([fr * xr - fi * xi, fr * xi + fi * xr], axis=1)
            mid = dot(prod.astype(BF16), inv[...])
            co, si = near_cos[...], near_sin[...]
            for n in range(2):
                parts = []
                for m in range(2):
                    top = (2 * n + m) * SIDE
                    re, im = mid[top : top + SIDE, :SPAN], mid[top : top + SIDE, SPAN:]
                    parts += [re * co - im * si, im * co + re * si]
                line = dot(near_last[...], jnp.concatenate(parts, axis=0).astype(BF16))
                for m in range(2):
                    for lanes in range(2):
                        back_wide[lanes, pl.ds(4 * i + 2 * n + m, SIDE, stride=OWN), :] = line[
                            m * SIDE : (m + 1) * SIDE, lanes * 128 : (lanes + 1) * 128
                        ]
            return carry

        lax.fori_loop(0, OWN // 4, four, 0)
        for lanes in range(2):
            work_b[:, :, pl.ds(lanes * 128, 128)] = (
                back_wide[lanes, pl.ds(0, SIDE * OWN)].astype(BF16).reshape(SIDE, OWN, 128)
            )

    def convolve(h, slot):
        for lanes in range(2):
            wide[lanes] = (
                recv_a[h, :, :, pl.ds(lanes * 128, 128)].astype(F32).reshape(PARTS * OWN, 128)
            )

        def channel_pair(i, carry):
            mids = []
            for n in range(2):
                c = 2 * i + n
                x = jnp.concatenate([column(wide, c), column(wide, HALF + c)], axis=0)
                mid = dot(pair[...], x.astype(BF16))
                mids += [twist(mid[: 2 * PARTS]), twist(mid[2 * PARTS :])]
            full = dot(jnp.concatenate(mids, axis=0), fwd[...])
            prods = []
            for n in range(2):
                f = spec[h * HALF + 2 * i + n]
                fr, fi = f[:, :SPAN], f[:, SPAN:]
                kv = full[2 * n * PARTS : (2 * n + 1) * PARTS]
                gg = full[(2 * n + 1) * PARTS : (2 * n + 2) * PARTS]
                kr, kj = kv[:, :SPAN], kv[:, SPAN:]
                gr, gj = gg[:, :SPAN], gg[:, SPAN:]
                prods += [
                    jnp.concatenate([fr * kr - fi * kj, fr * kj + fi * kr], axis=1),
                    jnp.concatenate([gr * fr + gj * fi, gj * fr - gr * fi], axis=1),
                    jnp.concatenate([gr * kr + gj * kj, gj * kr - gr * kj], axis=1),
                ]
            mid = dot(jnp.concatenate([q.astype(BF16) for q in prods], axis=0), inv[...])
            co, si = tcos[...], tsin[...]
            for n in range(2):
                c = 2 * i + n
                for a in range(3):
                    top = (3 * n + a) * PARTS
                    re, im = mid[top : top + PARTS, :SPAN], mid[top : top + PARTS, SPAN:]
                    y = jnp.concatenate([re * co - im * si, im * co + re * si], axis=0)
                    line = dot(last[...], y.astype(BF16))
                    for lanes in range(2):
                        piece = line[:, lanes * 128 : (lanes + 1) * 128]
                        if a < 2:
                            back_wide[lanes, pl.ds(a * HALF + c, PARTS, stride=OWN), :] = piece
                        else:
                            lag[slot, c // 4, lanes, pl.ds(c % 4, PARTS, stride=4), :] = piece
            return carry

        lax.fori_loop(0, HALF // 2, channel_pair, 0)
        here = pl.ds(pl.multiple_of(half * SIDE * OWN, OWN), SIDE * OWN)
        there = pl.ds(pl.multiple_of((1 - half) * SIDE * OWN, OWN), SIDE * OWN)
        chosen = []
        for lanes in range(2):
            send_b[h, :, :, pl.ds(lanes * 128, 128)] = (
                back_wide[lanes, here].astype(BF16).reshape(SIDE, OWN, 128)
            )
            pieces = back_wide[lanes, there].reshape(SIDE, 2, HALF, 128)
            chosen.append(jnp.where(half == 0, pieces[:, 0], pieces[:, 1]))
        send_c[h] = jnp.concatenate(chosen, axis=1).astype(BF16)

    def lag_swap(slot):
        return pltpu.make_async_remote_copy(
            src_ref=lag_out.at[slot],
            dst_ref=lag_in.at[slot],
            send_sem=ss_l.at[slot],
            recv_sem=rs_l.at[slot],
            device_id={"dp": other_core},
            device_id_type=MESH,
        )

    far = pltpu.make_async_remote_copy(
        src_ref=far_out,
        dst_ref=far_in,
        send_sem=ss_f.at[0],
        recv_sem=rs_f.at[0],
        device_id={"dp": other_cube},
        device_id_type=MESH,
    )

    for slot, h in enumerate(order):
        forward_whole(h).wait_recv()
        if slot == 1:
            lag_swap(0).wait_recv()
            far_out[...] = (lag[0, core] + lag_in[0].astype(F32)).astype(BF16)
            far.start()
        convolve(h, slot)
        send_planes(
            [
                (far_block(h), across), (return_block(h), beside),
                (far_block(h), behind), (return_block(h), z),
            ]
        )
        lag_out[slot] = lag[slot, 1 - core].astype(BF16)
        lag_swap(slot).start()
        if slot == 0:
            work_whole.wait_recv()
            work()
            send_planes([(work_result, beside), (work_result, z)])

    lag_swap(1).wait_recv()
    far.wait_recv()
    for lanes in range(2):
        total = lag[1, core, lanes] + lag_in[1, lanes].astype(F32) + far_in[lanes].astype(F32)
        for p in range(PARTS):
            out_filter[:, pl.ds(p * SPAN + lanes * 128, 128)] = total[4 * p : 4 * p + 4]

    for h in order:
        return_whole(h).wait_recv()
        far_whole(h).wait_recv()
    result_whole.wait_recv()

    def turn(rows):
        return dot_t(eye[...], rows.reshape(SPAN, SPAN).astype(BF16))

    for n in range(2):
        part = pl.ds(n * 16, 16)
        cols = pl.ds(pl.multiple_of((half * 2 + n) * SPAN, SPAN), SPAN)
        groups = [recv_b[h, part].astype(F32) for h in range(2)]
        for a, out in enumerate((out_conv, out_back)):
            rows = [g[:, a * HALF : (a + 1) * HALF] for g in groups]
            out[:, cols] = turn(jnp.concatenate(rows, axis=1)).astype(BF16)
        cols = pl.ds(pl.multiple_of(((1 - half) * 2 + n) * SPAN, SPAN), SPAN)
        rows = []
        for h in range(2):
            pieces = recv_c[h, part].astype(F32)
            rows.append(jnp.concatenate([pieces[:, :HALF], pieces[:, HALF:]], axis=2))
        owner = turn(jnp.concatenate(rows, axis=1))
        worker = turn(work_back[part])
        out_conv[:, cols] = jnp.where(half == 0, worker, owner).astype(BF16)
        out_back[:, cols] = jnp.where(half == 0, owner, worker).astype(BF16)

    for h in order:
        forward_whole(h).wait_send()
        return_whole(h).wait_send()
        far_whole(h).wait_send()
    work_whole.wait_send()
    result_whole.wait_send()
    for step in range(2):
        tap_copy(step).wait_send()
    for slot in range(2):
        lag_swap(slot).wait_send()
    far.wait_send()


def on_device(grad_out, gate, key_in, value_in, filters):
    vmem = pl.BlockSpec(memory_space=pltpu.VMEM)
    consts = [
        jnp.asarray(t.astype(np.float32) if n < 4 else np.asarray(t, dtype=jnp.bfloat16))
        for n, t in enumerate(tables())
    ]
    twists, (place, eye, *rest) = consts[:4], consts[4:]
    operands = (
        gate[0], key_in[0], value_in[0], grad_out[0], place, eye, filters, *twists, *rest,
    )
    dma = pltpu.SemaphoreType.DMA
    seq = jax.ShapeDtypeStruct((SPAN, 1024), BF16)
    conv, back, grad_filter = pl.pallas_call(
        kernel,
        out_shape=(seq, seq, jax.ShapeDtypeStruct((4, LENGTH), F32)),
        in_specs=[pl.BlockSpec(memory_space=pltpu.HBM)] * OPERANDS,
        out_specs=(vmem,) * 3,
        scratch_shapes=[
            *[pltpu.VMEM(x.shape, x.dtype) for x in operands],
            dma((OPERANDS,)),
            pltpu.VMEM((4, SPAN, 2 * SPAN), BF16),
            pltpu.VMEM((2, PARTS, OWN, SPAN), BF16),
            pltpu.VMEM((2, PARTS, OWN, SPAN), BF16),
            pltpu.VMEM((2, SIDE, OWN, SPAN), BF16),
            pltpu.VMEM((2, SIDE, OWN, SPAN), BF16),
            pltpu.VMEM((2, SIDE, OWN, 128), BF16),
            pltpu.VMEM((2, SIDE, OWN, 128), BF16),
            *[pltpu.VMEM((SIDE, OWN, SPAN), BF16)] * 4,
            pltpu.VMEM((OWN, LENGTH // 4), BF16),
            pltpu.VMEM((2, OWN, LENGTH // 4), BF16),
            pltpu.VMEM((2, PARTS * OWN, 128), F32),
            pltpu.VMEM((2, PARTS * OWN, 128), F32),
            pltpu.VMEM((OWN, PARTS, 2 * SPAN), F32),
            pltpu.VMEM((OWN, SIDE, 2 * SPAN), F32),
            pltpu.VMEM((2, 2, 2, PARTS * 4, 128), F32),
            pltpu.VMEM((2, 2, PARTS * 4, 128), BF16),
            pltpu.VMEM((2, 2, PARTS * 4, 128), BF16),
            pltpu.VMEM((2, PARTS * 4, 128), BF16),
            pltpu.VMEM((2, PARTS * 4, 128), BF16),
            *[dma((2,))] * 12, dma((1,)), dma((1,)),
        ],
        name="hyena_backward",
        compiler_params=pltpu.CompilerParams(
            collective_id=0, has_side_effects=True, vmem_limit_bytes=63 * 2**20
        ),
    )(*operands)
    wide = back.astype(F32)
    grad_gate = (grad_out[0].astype(F32) * conv.astype(F32)).astype(BF16)
    grad_key = (wide * value_in[0].astype(F32)).astype(BF16)
    grad_value = (wide * key_in[0].astype(F32)).astype(BF16)
    return (grad_gate[None], grad_key[None], grad_value[None], grad_filter)


def solution(mesh):
    return jax.shard_map(
        on_device,
        mesh=mesh,
        in_specs=(
            P("dp", "context", None),
            P("dp", "context", None),
            P("dp", "context", None),
            P("dp", "context", None),
            P("context", None),
        ),
        out_specs=(
            P("dp", "context", None),
            P("dp", "context", None),
            P("dp", "context", None),
            P(("context", "dp"), None),
        ),
        check_vma=False,
    )
```

```python
import functools

import jax
import jax.numpy as jnp
import numpy as np
from jax import lax
from jax.experimental import pallas as pl
from jax.experimental.pallas import tpu as pltpu
from jax.sharding import PartitionSpec as P

MESH = pl.DeviceIdType.MESH
F32 = jnp.float32
BF16 = jnp.bfloat16

SPAN = 256
PARTS = 64
OWN = 16
HALF = 8
LENGTH = SPAN * PARTS
SIDE = PARTS // 2
OPERANDS = 18


def tables():
    k1 = np.arange(PARTS)[:, None] + 0.25
    p = np.arange(PARTS)[None, :]
    angle = 2 * np.pi * k1 * p / PARTS
    first = np.concatenate([np.cos(angle), -np.sin(angle)], 0)
    zero = np.zeros_like(first)
    pair = np.block([[first, zero], [zero, first]])
    filt = np.concatenate([first, first], 1)
    last = np.concatenate([np.cos(angle).T, -np.sin(angle).T], 1) / LENGTH
    s = np.arange(SPAN)
    twist = 2 * np.pi * k1 * s[None, :] / LENGTH
    grid = 2 * np.pi * (s[:, None] * s[None, :] % SPAN) / SPAN
    cos, sin = np.cos(grid), np.sin(grid)
    forward = np.block([[cos, -sin], [sin, cos]])
    inverse = np.block([[cos, sin], [-sin, cos]])
    place = np.zeros((2, SPAN, 2 * SPAN))
    for h in range(2):
        for j in range(SPAN // OWN):
            for a in range(2):
                for c in range(HALF):
                    place[h, j * OWN + a * HALF + c, a * SPAN + j * OWN + h * HALF + c] = 1
    eye = np.eye(SPAN)
    k1 = np.arange(SIDE)[:, None] + 0.25
    angle = 2 * np.pi * k1 * np.arange(SIDE)[None, :] / SIDE
    first = np.concatenate([np.cos(angle), -np.sin(angle)], 0)
    near = np.block([[first, np.zeros_like(first)], [np.zeros_like(first), first]])
    final = np.concatenate([np.cos(angle).T, -np.sin(angle).T], 1) * 2 / LENGTH
    near_last = np.block([[final, np.zeros_like(final)], [np.zeros_like(final), final]])
    near_twist = 2 * np.pi * k1 * s[None, :] * 2 / LENGTH
    return (
        np.cos(twist), np.sin(twist), np.cos(near_twist), np.sin(near_twist),
        place, eye, filt, forward, near, pair, inverse, last, near_last,
    )


def dot(a, b):
    return jnp.dot(a, b, preferred_element_type=F32)


def dot_t(a, b):
    return lax.dot_general(a, b, (((1,), (1,)), ((), ())), preferred_element_type=F32)


def target(me, plane, k):
    x, y = (me // 4) % 4, me % 4
    return plane * 16 + ((x + k // 4) % 4) * 4 + (y + k % 4) % 4


def kernel(*refs):
    given, refs = refs[:OPERANDS], refs[OPERANDS:]
    results, refs = refs[:3], refs[3:]
    held, loaded, refs = refs[:OPERANDS], refs[OPERANDS], refs[OPERANDS + 1 :]
    loads = [
        pltpu.make_async_copy(src, dst, loaded.at[n])
        for n, (src, dst) in enumerate(zip(given, held))
    ]
    for load in loads:
        load.start()
    body(loads, *held, *results, *refs)


def body(
    loads,
    gt, ki, vi, go, place, eye, flt, tcos, tsin, near_cos, near_sin,
    filt, fwd, near, pair, inv, last, near_last,
    out_conv, out_back, out_filter,
    both, send_a, recv_a, send_b, recv_b, send_c, recv_c, work_a, work_in, work_b, work_back,
    taps, near_taps, wide, back_wide, spec, near_spec, lag, lag_out, lag_in, far_out, far_in,
    ss_a, rs_a, ss_b, rs_b, ss_c, rs_c, ss_w, rs_w, ss_t, rs_t, ss_l, rs_l, ss_f, rs_f, cross,
):
    dp, me = lax.axis_index("dp"), lax.axis_index("context")
    z_hi, core = dp // 2, dp % 2
    other_core = z_hi * 2 + (1 - core)
    other_cube = (1 - z_hi) * 2 + core

    barrier = pltpu.get_barrier_semaphore()

    z = me // 16
    half, odd = z // 2, z % 2
    across, behind = (1 - half) * 2 + odd, (1 - half) * 2 + (1 - odd)
    beside = half * 2 + (1 - odd)
    planes = (across, behind, beside, z)

    for plane in planes:

        def greet(k, carry, plane=plane):
            pl.semaphore_signal(
                barrier, inc=1, device_id={"context": target(me, plane, k)}, device_id_type=MESH
            )
            return carry

        lax.fori_loop(1 if plane is z else 0, 16, greet, 0)
    pl.semaphore_signal(barrier, inc=1, device_id={"dp": other_core}, device_id_type=MESH)
    twin = {"dp": other_cube, "context": (me + SIDE) % PARTS}
    partners = ({"dp": other_cube}, twin)

    for load in loads[:7]:
        load.wait()
    order = (1 - z_hi, z_hi)

    def rows_of(h, plane):
        rows = dot_t(place[h], both[plane]).astype(BF16)
        send_a[h, pl.ds(plane * 16, 16)] = rows.reshape(16, OWN, SPAN)

    mine = me % SIDE

    def forward_block(h):
        return lambda d: (send_a.at[h, d], recv_a.at[h, me], ss_a.at[h], rs_a.at[h])

    def work_block(d):
        return work_a.at[d % SIDE], work_in.at[mine], ss_w.at[0], rs_w.at[0]

    def return_block(h):
        return lambda d: (send_b.at[h, d % SIDE], recv_b.at[h, mine], ss_b.at[h], rs_b.at[h])

    def far_block(h):
        return lambda d: (send_c.at[h, d % SIDE], recv_c.at[h, mine], ss_c.at[h], rs_c.at[h])

    def work_result(d):
        return work_b.at[d % SIDE], work_back.at[mine], ss_w.at[1], rs_w.at[1]

    def send(block, plane, k):
        d = target(me, plane, k)
        src, dst, ssem, rsem = block(d)
        pltpu.make_async_remote_copy(
            src_ref=src,
            dst_ref=dst,
            send_sem=ssem,
            recv_sem=rsem,
            device_id={"context": d},
            device_id_type=MESH,
        ).start()

    def send_planes(jobs):
        def one(k, carry):
            for block, plane in jobs:
                send(block, plane, k)
            return carry

        lax.fori_loop(1, 16, one, 0)
        for block, plane in jobs:
            if plane is z:
                src, dst, _, _ = block(me)
                dst[...] = src[...]
            else:
                send(block, plane, 0)

    def tap_copy(step):
        here = near_taps.at[core]
        return pltpu.make_async_remote_copy(
            src_ref=taps if step == 0 else here,
            dst_ref=here,
            send_sem=ss_t.at[step],
            recv_sem=rs_t.at[step],
            device_id=twin if step == 0 else {"dp": other_core},
            device_id_type=MESH,
        )

    first, second = order
    for n, plane in enumerate(planes):
        cols = pl.ds(pl.multiple_of(plane * SPAN, SPAN), SPAN)
        kv = (ki[:, cols].astype(F32) * vi[:, cols].astype(F32)).astype(BF16)
        gg = (go[:, cols].astype(F32) * gt[:, cols].astype(F32)).astype(BF16)
        both[plane] = jnp.concatenate([kv, gg], axis=1)
        rows_of(first, plane)
        if n == 0:
            taps[...] = flt[
                :, pl.ds(pl.multiple_of(core * (LENGTH // 4), LENGTH // 4), LENGTH // 4)
            ].astype(BF16)
            pl.semaphore_wait(barrier, PARTS + 2 * z_hi)

            @pl.when(z_hi == 0)
            def _():
                for partner in partners:
                    pl.semaphore_signal(barrier, inc=1, device_id=partner, device_id_type=MESH)

            @pl.when(z_hi == 1)
            def _():
                for partner in partners:
                    pl.semaphore_signal(cross, inc=1, device_id=partner, device_id_type=MESH)
                tap_copy(0).start()

            send_planes([(forward_block(first), plane)])
    send_planes([(forward_block(first), p) for p in (beside, behind, z)])

    @pl.when(z_hi == 0)
    def _():
        pl.semaphore_wait(cross, 2)
        tap_copy(0).start()

    rows_of(second, across)
    rows_of(second, behind)
    for n in range(2):
        one_array = both[(1 - half) * 2 + n, :, pl.ds(pl.multiple_of(half * SPAN, SPAN), SPAN)]
        work_a[pl.ds(n * 16, 16)] = dot_t(eye[...], one_array).astype(BF16).reshape(16, OWN, SPAN)
    send_planes(
        [
            (forward_block(second), across), (work_block, beside),
            (forward_block(second), behind), (work_block, z),
        ]
    )
    rows_of(second, beside)
    rows_of(second, z)
    send_planes([(forward_block(second), beside), (forward_block(second), z)])

    def whole(src, dst, count, ssem, rsem):
        return pltpu.make_async_remote_copy(
            src_ref=src.at[pl.ds(0, count)],
            dst_ref=dst.at[pl.ds(0, count)],
            send_sem=ssem,
            recv_sem=rsem,
            device_id={"context": me},
            device_id_type=MESH,
        )

    def forward_whole(h):
        return whole(send_a.at[h], recv_a.at[h], PARTS - 1, ss_a.at[h], rs_a.at[h])

    def return_whole(h):
        return whole(send_b.at[h], recv_b.at[h], SIDE - 1, ss_b.at[h], rs_b.at[h])

    def far_whole(h):
        return whole(send_c.at[h], recv_c.at[h], SIDE, ss_c.at[h], rs_c.at[h])

    work_whole = whole(work_a, work_in, SIDE - 1, ss_w.at[0], rs_w.at[0])
    result_whole = whole(work_b, work_back, SIDE - 1, ss_w.at[1], rs_w.at[1])

    for load in loads[7:]:
        load.wait()

    def lay(p, carry):
        cols = pl.ds(pl.multiple_of(p * SPAN, SPAN), SPAN)
        for lanes in range(2):
            wide[lanes, pl.ds(pl.multiple_of(p * OWN, OWN), OWN), :] = flt[
                :, pl.ds(pl.multiple_of(p * SPAN + lanes * 128, 128), 128)
            ]
        return carry

    lax.fori_loop(0, PARTS, lay, 0)

    def column(ref, row, parts=PARTS):
        return jnp.concatenate(
            [ref[lanes, pl.ds(row, parts, stride=OWN), :] for lanes in range(2)], axis=1
        )

    def twist(mid, cos=tcos, sin=tsin):
        parts = cos.shape[0]
        re, im = mid[:parts], mid[parts:]
        c, s = cos[...], sin[...]
        return jnp.concatenate([re * c + im * s, im * c - re * s], axis=1).astype(BF16)

    def filter_pair(i, carry):
        mids = []
        for n in range(2):
            x = column(wide, 2 * i + n)
            high = x.astype(BF16)
            low = (x - high.astype(F32)).astype(BF16)
            mids.append(twist(dot(filt[...], jnp.concatenate([high, low], axis=0))))
        full = dot(jnp.concatenate(mids, axis=0), fwd[...])
        spec[pl.ds(2 * i, 2)] = full.reshape(2, PARTS, 2 * SPAN)
        return carry

    lax.fori_loop(0, OWN // 2, filter_pair, 0)

    def near_rows(i):
        mids = []
        for n in range(2):
            x = [column(wide, 4 * i + 2 * n + m, SIDE) for m in range(2)]
            mid = dot(near[...], jnp.concatenate(x, axis=0).astype(BF16))
            for m in range(2):
                mids.append(twist(mid[2 * m * SIDE : 2 * (m + 1) * SIDE], near_cos, near_sin))
        return dot(jnp.concatenate(mids, axis=0), fwd[...])

    def near_filters(i, carry):
        full = near_rows(i)
        im = jnp.where(half == 0, full[:, SPAN:], -full[:, SPAN:])
        full = jnp.concatenate([full[:, :SPAN], im], axis=1)
        near_spec[pl.ds(4 * i, 4)] = full.reshape(4, SIDE, 2 * SPAN)
        return carry

    def near_spectrum():
        for q in range(2):
            for p in range(SIDE // 2):
                for lanes in range(2):
                    wide[lanes, pl.ds((q * SIDE // 2 + p) * OWN, OWN), :] = near_taps[
                        q, :, pl.ds(p * SPAN + lanes * 128, 128)
                    ].astype(F32)
        lax.fori_loop(0, OWN // 4, near_filters, 0)

    def work():
        for lanes in range(2):
            wide[lanes, pl.ds(0, SIDE * OWN)] = (
                work_in[:, :, pl.ds(lanes * 128, 128)].astype(F32).reshape(SIDE * OWN, 128)
            )

        def four(i, carry):
            x = near_rows(i)
            f = near_spec[pl.ds(4 * i, 4)].reshape(4 * SIDE, 2 * SPAN)
            fr, fi = f[:, :SPAN], f[:, SPAN:]
            xr, xi = x[:, :SPAN], x[:, SPAN:]
            prod = jnp.concatenate([fr * xr - fi * xi, fr * xi + fi * xr], axis=1)
            mid = dot(prod.astype(BF16), inv[...])
            co, si = near_cos[...], near_sin[...]
            for n in range(2):
                parts = []
                for m in range(2):
                    top = (2 * n + m) * SIDE
                    re, im = mid[top : top + SIDE, :SPAN], mid[top : top + SIDE, SPAN:]
                    parts += [re * co - im * si, im * co + re * si]
                line = dot(near_last[...], jnp.concatenate(parts, axis=0).astype(BF16))
                for m in range(2):
                    for lanes in range(2):
                        back_wide[lanes, pl.ds(4 * i + 2 * n + m, SIDE, stride=OWN), :] = line[
                            m * SIDE : (m + 1) * SIDE, lanes * 128 : (lanes + 1) * 128
                        ]
            return carry

        lax.fori_loop(0, OWN // 4, four, 0)
        for lanes in range(2):
            work_b[:, :, pl.ds(lanes * 128, 128)] = (
                back_wide[lanes, pl.ds(0, SIDE * OWN)].astype(BF16).reshape(SIDE, OWN, 128)
            )

    def convolve(h, slot):
        for lanes in range(2):
            wide[lanes] = (
                recv_a[h, :, :, pl.ds(lanes * 128, 128)].astype(F32).reshape(PARTS * OWN, 128)
            )

        def channel_pair(i, carry):
            mids = []
            for n in range(2):
                c = 2 * i + n
                x = jnp.concatenate([column(wide, c), column(wide, HALF + c)], axis=0)
                mid = dot(pair[...], x.astype(BF16))
                mids += [twist(mid[: 2 * PARTS]), twist(mid[2 * PARTS :])]
            full = dot(jnp.concatenate(mids, axis=0), fwd[...])
            prods = []
            for n in range(2):
                f = spec[h * HALF + 2 * i + n]
                fr, fi = f[:, :SPAN], f[:, SPAN:]
                kv = full[2 * n * PARTS : (2 * n + 1) * PARTS]
                gg = full[(2 * n + 1) * PARTS : (2 * n + 2) * PARTS]
                kr, kj = kv[:, :SPAN], kv[:, SPAN:]
                gr, gj = gg[:, :SPAN], gg[:, SPAN:]
                prods += [
                    jnp.concatenate([fr * kr - fi * kj, fr * kj + fi * kr], axis=1),
                    jnp.concatenate([gr * fr + gj * fi, gj * fr - gr * fi], axis=1),
                    jnp.concatenate([gr * kr + gj * kj, gj * kr - gr * kj], axis=1),
                ]
            mid = dot(jnp.concatenate([q.astype(BF16) for q in prods], axis=0), inv[...])
            co, si = tcos[...], tsin[...]
            for n in range(2):
                c = 2 * i + n
                for a in range(3):
                    top = (3 * n + a) * PARTS
                    re, im = mid[top : top + PARTS, :SPAN], mid[top : top + PARTS, SPAN:]
                    y = jnp.concatenate([re * co - im * si, im * co + re * si], axis=0)
                    line = dot(last[...], y.astype(BF16))
                    for lanes in range(2):
                        piece = line[:, lanes * 128 : (lanes + 1) * 128]
                        if a < 2:
                            back_wide[lanes, pl.ds(a * HALF + c, PARTS, stride=OWN), :] = piece
                        else:
                            lag[slot, c // 4, lanes, pl.ds(c % 4, PARTS, stride=4), :] = piece
            return carry

        lax.fori_loop(0, HALF // 2, channel_pair, 0)
        here = pl.ds(pl.multiple_of(half * SIDE * OWN, OWN), SIDE * OWN)
        there = pl.ds(pl.multiple_of((1 - half) * SIDE * OWN, OWN), SIDE * OWN)
        chosen = []
        for lanes in range(2):
            send_b[h, :, :, pl.ds(lanes * 128, 128)] = (
                back_wide[lanes, here].astype(BF16).reshape(SIDE, OWN, 128)
            )
            pieces = back_wide[lanes, there].reshape(SIDE, 2, HALF, 128)
            chosen.append(jnp.where(half == 0, pieces[:, 0], pieces[:, 1]))
        send_c[h] = jnp.concatenate(chosen, axis=1).astype(BF16)

    def lag_swap(slot):
        return pltpu.make_async_remote_copy(
            src_ref=lag_out.at[slot],
            dst_ref=lag_in.at[slot],
            send_sem=ss_l.at[slot],
            recv_sem=rs_l.at[slot],
            device_id={"dp": other_core},
            device_id_type=MESH,
        )

    far = pltpu.make_async_remote_copy(
        src_ref=far_out,
        dst_ref=far_in,
        send_sem=ss_f.at[0],
        recv_sem=rs_f.at[0],
        device_id={"dp": other_cube},
        device_id_type=MESH,
    )

    for slot, h in enumerate(order):
        forward_whole(h).wait_recv()
        if slot == 1:
            lag_swap(0).wait_recv()
            far_out[...] = (lag[0, core] + lag_in[0].astype(F32)).astype(BF16)
            far.start()
        else:
            tap_copy(0).wait_recv()
            tap_copy(1).start()
        convolve(h, slot)
        send_planes(
            [
                (far_block(h), across), (return_block(h), beside),
                (far_block(h), behind), (return_block(h), z),
            ]
        )
        lag_out[slot] = lag[slot, 1 - core].astype(BF16)
        lag_swap(slot).start()
        if slot == 0:
            tap_copy(1).wait_recv()
            near_spectrum()
            work_whole.wait_recv()
            work()
            send_planes([(work_result, beside), (work_result, z)])

    lag_swap(1).wait_recv()
    far.wait_recv()
    for lanes in range(2):
        total = lag[1, core, lanes] + lag_in[1, lanes].astype(F32) + far_in[lanes].astype(F32)
        for p in range(PARTS):
            out_filter[:, pl.ds(p * SPAN + lanes * 128, 128)] = total[4 * p : 4 * p + 4]

    for h in order:
        return_whole(h).wait_recv()
        far_whole(h).wait_recv()
    result_whole.wait_recv()

    def turn(rows):
        return dot_t(eye[...], rows.reshape(SPAN, SPAN).astype(BF16))

    for n in range(2):
        part = pl.ds(n * 16, 16)
        cols = pl.ds(pl.multiple_of((half * 2 + n) * SPAN, SPAN), SPAN)
        groups = [recv_b[h, part].astype(F32) for h in range(2)]
        for a, out in enumerate((out_conv, out_back)):
            rows = [g[:, a * HALF : (a + 1) * HALF] for g in groups]
            out[:, cols] = turn(jnp.concatenate(rows, axis=1)).astype(BF16)
        cols = pl.ds(pl.multiple_of(((1 - half) * 2 + n) * SPAN, SPAN), SPAN)
        rows = []
        for h in range(2):
            pieces = recv_c[h, part].astype(F32)
            rows.append(jnp.concatenate([pieces[:, :HALF], pieces[:, HALF:]], axis=2))
        owner = turn(jnp.concatenate(rows, axis=1))
        worker = turn(work_back[part])
        out_conv[:, cols] = jnp.where(half == 0, worker, owner).astype(BF16)
        out_back[:, cols] = jnp.where(half == 0, owner, worker).astype(BF16)

    for h in order:
        forward_whole(h).wait_send()
        return_whole(h).wait_send()
        far_whole(h).wait_send()
    work_whole.wait_send()
    result_whole.wait_send()
    for step in range(2):
        tap_copy(step).wait_send()
    for slot in range(2):
        lag_swap(slot).wait_send()
    far.wait_send()


def on_device(grad_out, gate, key_in, value_in, filters):
    vmem = pl.BlockSpec(memory_space=pltpu.VMEM)
    consts = [
        jnp.asarray(t.astype(np.float32) if n < 4 else np.asarray(t, dtype=jnp.bfloat16))
        for n, t in enumerate(tables())
    ]
    twists, (place, eye, *rest) = consts[:4], consts[4:]
    operands = (
        gate[0], key_in[0], value_in[0], grad_out[0], place, eye, filters, *twists, *rest,
    )
    dma = pltpu.SemaphoreType.DMA
    seq = jax.ShapeDtypeStruct((SPAN, 1024), BF16)
    conv, back, grad_filter = pl.pallas_call(
        kernel,
        out_shape=(seq, seq, jax.ShapeDtypeStruct((4, LENGTH), F32)),
        in_specs=[pl.BlockSpec(memory_space=pltpu.HBM)] * OPERANDS,
        out_specs=(vmem,) * 3,
        scratch_shapes=[
            *[pltpu.VMEM(x.shape, x.dtype) for x in operands],
            dma((OPERANDS,)),
            pltpu.VMEM((4, SPAN, 2 * SPAN), BF16),
            pltpu.VMEM((2, PARTS, OWN, SPAN), BF16),
            pltpu.VMEM((2, PARTS, OWN, SPAN), BF16),
            pltpu.VMEM((2, SIDE, OWN, SPAN), BF16),
            pltpu.VMEM((2, SIDE, OWN, SPAN), BF16),
            pltpu.VMEM((2, SIDE, OWN, 128), BF16),
            pltpu.VMEM((2, SIDE, OWN, 128), BF16),
            *[pltpu.VMEM((SIDE, OWN, SPAN), BF16)] * 4,
            pltpu.VMEM((OWN, LENGTH // 4), BF16),
            pltpu.VMEM((2, OWN, LENGTH // 4), BF16),
            pltpu.VMEM((2, PARTS * OWN, 128), F32),
            pltpu.VMEM((2, PARTS * OWN, 128), F32),
            pltpu.VMEM((OWN, PARTS, 2 * SPAN), F32),
            pltpu.VMEM((OWN, SIDE, 2 * SPAN), F32),
            pltpu.VMEM((2, 2, 2, PARTS * 4, 128), F32),
            pltpu.VMEM((2, 2, PARTS * 4, 128), BF16),
            pltpu.VMEM((2, 2, PARTS * 4, 128), BF16),
            pltpu.VMEM((2, PARTS * 4, 128), BF16),
            pltpu.VMEM((2, PARTS * 4, 128), BF16),
            *[dma((2,))] * 12, dma((1,)), dma((1,)),
            pltpu.SemaphoreType.REGULAR,
        ],
        name="hyena_backward",
        compiler_params=pltpu.CompilerParams(
            collective_id=0, has_side_effects=True, vmem_limit_bytes=58 * 2**20
        ),
    )(*operands)
    wide = back.astype(F32)
    grad_gate = (grad_out[0].astype(F32) * conv.astype(F32)).astype(BF16)
    grad_key = (wide * value_in[0].astype(F32)).astype(BF16)
    grad_value = (wide * key_in[0].astype(F32)).astype(BF16)
    return (grad_gate[None], grad_key[None], grad_value[None], grad_filter)


def solution(mesh):
    return jax.shard_map(
        on_device,
        mesh=mesh,
        in_specs=(
            P("dp", "context", None),
            P("dp", "context", None),
            P("dp", "context", None),
            P("dp", "context", None),
            P("context", None),
        ),
        out_specs=(
            P("dp", "context", None),
            P("dp", "context", None),
            P("dp", "context", None),
            P(("context", "dp"), None),
        ),
        check_vma=False,
    )
```

```python
import functools

import jax
import jax.numpy as jnp
import numpy as np
from jax import lax
from jax.experimental import pallas as pl
from jax.experimental.pallas import tpu as pltpu
from jax.sharding import PartitionSpec as P

MESH = pl.DeviceIdType.MESH
F32 = jnp.float32
BF16 = jnp.bfloat16

SPAN = 256
PARTS = 64
OWN = 16
HALF = 8
LENGTH = SPAN * PARTS
SIDE = PARTS // 2
OPERANDS = 18


def tables():
    k1 = np.arange(PARTS)[:, None] + 0.25
    p = np.arange(PARTS)[None, :]
    angle = 2 * np.pi * k1 * p / PARTS
    first = np.concatenate([np.cos(angle), -np.sin(angle)], 0)
    zero = np.zeros_like(first)
    pair = np.block([[first, zero], [zero, first]])
    filt = np.concatenate([first, first], 1)
    last = np.concatenate([np.cos(angle).T, -np.sin(angle).T], 1) / LENGTH
    s = np.arange(SPAN)
    twist = 2 * np.pi * k1 * s[None, :] / LENGTH
    grid = 2 * np.pi * (s[:, None] * s[None, :] % SPAN) / SPAN
    cos, sin = np.cos(grid), np.sin(grid)
    forward = np.block([[cos, -sin], [sin, cos]])
    inverse = np.block([[cos, sin], [-sin, cos]])
    place = np.zeros((2, SPAN, 2 * SPAN))
    for h in range(2):
        for j in range(SPAN // OWN):
            for a in range(2):
                for c in range(HALF):
                    place[h, j * OWN + a * HALF + c, a * SPAN + j * OWN + h * HALF + c] = 1
    eye = np.eye(SPAN)
    k1 = np.arange(SIDE)[:, None] + 0.25
    angle = 2 * np.pi * k1 * np.arange(SIDE)[None, :] / SIDE
    first = np.concatenate([np.cos(angle), -np.sin(angle)], 0)
    near = np.block([[first, np.zeros_like(first)], [np.zeros_like(first), first]])
    final = np.concatenate([np.cos(angle).T, -np.sin(angle).T], 1) * 2 / LENGTH
    near_last = np.block([[final, np.zeros_like(final)], [np.zeros_like(final), final]])
    near_twist = 2 * np.pi * k1 * s[None, :] * 2 / LENGTH
    return (
        np.cos(twist), np.sin(twist), np.cos(near_twist), np.sin(near_twist),
        place, eye, filt, forward, near, pair, inverse, last, near_last,
    )


def dot(a, b):
    return jnp.dot(a, b, preferred_element_type=F32)


def dot_t(a, b):
    return lax.dot_general(a, b, (((1,), (1,)), ((), ())), preferred_element_type=F32)


def target(me, plane, k):
    x, y = (me // 4) % 4, me % 4
    return plane * 16 + ((x + k // 4) % 4) * 4 + (y + k % 4) % 4


def kernel(*refs):
    given, refs = refs[:OPERANDS], refs[OPERANDS:]
    results, refs = refs[:4], refs[4:]
    held, loaded, refs = refs[:OPERANDS], refs[OPERANDS], refs[OPERANDS + 1 :]
    loads = [
        pltpu.make_async_copy(src, dst, loaded.at[n])
        for n, (src, dst) in enumerate(zip(given, held))
    ]
    for load in loads:
        load.start()
    body(loads, *held, *results, *refs)


def body(
    loads,
    gt, ki, vi, go, place, eye, flt, tcos, tsin, near_cos, near_sin,
    filt, fwd, near, pair, inv, last, near_last,
    recv_b, recv_c, work_back, out_filter,
    both, send_a, recv_a, send_b, send_c, work_a, work_in, work_b,
    taps, near_taps, wide, back_wide, spec, near_spec, lag, lag_out, lag_in, far_out, far_in, lag_sum,
    ss_a, rs_a, ss_b, rs_b, ss_c, rs_c, ss_w, rs_w, ss_t, rs_t, ss_l, rs_l, ss_f, rs_f, kept, cross,
):
    dp, me = lax.axis_index("dp"), lax.axis_index("context")
    z_hi, core = dp // 2, dp % 2
    other_core = z_hi * 2 + (1 - core)
    other_cube = (1 - z_hi) * 2 + core

    barrier = pltpu.get_barrier_semaphore()

    z = me // 16
    half, odd = z // 2, z % 2
    across, behind = (1 - half) * 2 + odd, (1 - half) * 2 + (1 - odd)
    beside = half * 2 + (1 - odd)
    planes = (across, behind, beside, z)

    for plane in planes:

        def greet(k, carry, plane=plane):
            pl.semaphore_signal(
                barrier, inc=1, device_id={"context": target(me, plane, k)}, device_id_type=MESH
            )
            return carry

        lax.fori_loop(1 if plane is z else 0, 16, greet, 0)
    pl.semaphore_signal(barrier, inc=1, device_id={"dp": other_core}, device_id_type=MESH)
    twin = {"dp": other_cube, "context": (me + SIDE) % PARTS}
    partners = ({"dp": other_cube}, twin)

    for load in loads[:7]:
        load.wait()
    order = (1 - z_hi, z_hi)

    def rows_of(h, plane):
        rows = dot_t(place[h], both[plane]).astype(BF16)
        send_a[h, pl.ds(plane * 16, 16)] = rows.reshape(16, OWN, SPAN)

    mine = me % SIDE

    def forward_block(h):
        return lambda d: (send_a.at[h, d], recv_a.at[h, me], ss_a.at[h], rs_a.at[h], None)

    def work_block(d):
        return work_a.at[d % SIDE], work_in.at[mine], ss_w.at[0], rs_w.at[0], None

    def return_block(h):
        return lambda d: (
            send_b.at[h, d % SIDE], recv_b.at[h, mine], ss_b.at[h], rs_b.at[h], kept.at[h],
        )

    def far_block(h):
        return lambda d: (send_c.at[h, d % SIDE], recv_c.at[h, mine], ss_c.at[h], rs_c.at[h], None)

    def work_result(d):
        return work_b.at[d % SIDE], work_back.at[mine], ss_w.at[1], rs_w.at[1], kept.at[2]

    def send(block, plane, k):
        d = target(me, plane, k)
        src, dst, ssem, rsem, _ = block(d)
        pltpu.make_async_remote_copy(
            src_ref=src,
            dst_ref=dst,
            send_sem=ssem,
            recv_sem=rsem,
            device_id={"context": d},
            device_id_type=MESH,
        ).start()

    def send_planes(jobs):
        def one(k, carry):
            for block, plane in jobs:
                send(block, plane, k)
            return carry

        lax.fori_loop(1, 16, one, 0)
        for block, plane in jobs:
            if plane is z:
                src, dst, _, _, own = block(me)
                if own is None:
                    dst[...] = src[...]
                else:
                    pltpu.make_async_copy(src, dst, own).start()
            else:
                send(block, plane, 0)

    def tap_copy(step):
        here = near_taps.at[core]
        return pltpu.make_async_remote_copy(
            src_ref=taps if step == 0 else here,
            dst_ref=here,
            send_sem=ss_t.at[step],
            recv_sem=rs_t.at[step],
            device_id=twin if step == 0 else {"dp": other_core},
            device_id_type=MESH,
        )

    first, second = order
    for n, plane in enumerate(planes):
        cols = pl.ds(pl.multiple_of(plane * SPAN, SPAN), SPAN)
        kv = (ki[:, cols].astype(F32) * vi[:, cols].astype(F32)).astype(BF16)
        gg = (go[:, cols].astype(F32) * gt[:, cols].astype(F32)).astype(BF16)
        both[plane] = jnp.concatenate([kv, gg], axis=1)
        rows_of(first, plane)
        if n == 0:
            taps[...] = flt[
                :, pl.ds(pl.multiple_of(core * (LENGTH // 4), LENGTH // 4), LENGTH // 4)
            ].astype(BF16)
            pl.semaphore_wait(barrier, PARTS + 2 * z_hi)

            @pl.when(z_hi == 0)
            def _():
                for partner in partners:
                    pl.semaphore_signal(barrier, inc=1, device_id=partner, device_id_type=MESH)

            @pl.when(z_hi == 1)
            def _():
                for partner in partners:
                    pl.semaphore_signal(cross, inc=1, device_id=partner, device_id_type=MESH)
                tap_copy(0).start()

            send_planes([(forward_block(first), plane)])
    send_planes([(forward_block(first), p) for p in (beside, behind, z)])

    @pl.when(z_hi == 0)
    def _():
        pl.semaphore_wait(cross, 2)
        tap_copy(0).start()

    rows_of(second, across)
    rows_of(second, behind)
    for n in range(2):
        one_array = both[(1 - half) * 2 + n, :, pl.ds(pl.multiple_of(half * SPAN, SPAN), SPAN)]
        work_a[pl.ds(n * 16, 16)] = dot_t(eye[...], one_array).astype(BF16).reshape(16, OWN, SPAN)
    send_planes(
        [
            (forward_block(second), across), (work_block, beside),
            (forward_block(second), behind), (work_block, z),
        ]
    )
    rows_of(second, beside)
    rows_of(second, z)
    send_planes([(forward_block(second), beside), (forward_block(second), z)])

    def whole(src, dst, count, ssem, rsem):
        return pltpu.make_async_remote_copy(
            src_ref=src.at[pl.ds(0, count)],
            dst_ref=dst.at[pl.ds(0, count)],
            send_sem=ssem,
            recv_sem=rsem,
            device_id={"context": me},
            device_id_type=MESH,
        )

    def forward_whole(h):
        return whole(send_a.at[h], recv_a.at[h], PARTS - 1, ss_a.at[h], rs_a.at[h])

    def return_whole(h):
        return whole(send_b.at[h], recv_b.at[h], SIDE - 1, ss_b.at[h], rs_b.at[h])

    def far_whole(h):
        return whole(send_c.at[h], recv_c.at[h], SIDE, ss_c.at[h], rs_c.at[h])

    work_whole = whole(work_a, work_in, SIDE - 1, ss_w.at[0], rs_w.at[0])
    result_whole = whole(work_b, work_back, SIDE - 1, ss_w.at[1], rs_w.at[1])

    for load in loads[7:]:
        load.wait()

    def lay(p, carry):
        cols = pl.ds(pl.multiple_of(p * SPAN, SPAN), SPAN)
        for lanes in range(2):
            wide[lanes, pl.ds(pl.multiple_of(p * OWN, OWN), OWN), :] = flt[
                :, pl.ds(pl.multiple_of(p * SPAN + lanes * 128, 128), 128)
            ]
        return carry

    lax.fori_loop(0, PARTS, lay, 0)

    def column(ref, row, parts=PARTS):
        return jnp.concatenate(
            [ref[lanes, pl.ds(row, parts, stride=OWN), :] for lanes in range(2)], axis=1
        )

    def twist(mid, cos=tcos, sin=tsin):
        parts = cos.shape[0]
        re, im = mid[:parts], mid[parts:]
        c, s = cos[...], sin[...]
        return jnp.concatenate([re * c + im * s, im * c - re * s], axis=1).astype(BF16)

    def filter_pair(i, carry):
        mids = []
        for n in range(2):
            x = column(wide, 2 * i + n)
            high = x.astype(BF16)
            low = (x - high.astype(F32)).astype(BF16)
            mids.append(twist(dot(filt[...], jnp.concatenate([high, low], axis=0))))
        full = dot(jnp.concatenate(mids, axis=0), fwd[...])
        spec[pl.ds(2 * i, 2)] = full.reshape(2, PARTS, 2 * SPAN)
        return carry

    lax.fori_loop(0, OWN // 2, filter_pair, 0)

    def near_rows(i):
        mids = []
        for n in range(2):
            x = [column(wide, 4 * i + 2 * n + m, SIDE) for m in range(2)]
            mid = dot(near[...], jnp.concatenate(x, axis=0).astype(BF16))
            for m in range(2):
                mids.append(twist(mid[2 * m * SIDE : 2 * (m + 1) * SIDE], near_cos, near_sin))
        return dot(jnp.concatenate(mids, axis=0), fwd[...])

    def near_filters(i, carry):
        full = near_rows(i)
        im = jnp.where(half == 0, full[:, SPAN:], -full[:, SPAN:])
        full = jnp.concatenate([full[:, :SPAN], im], axis=1)
        near_spec[pl.ds(4 * i, 4)] = full.reshape(4, SIDE, 2 * SPAN)
        return carry

    def near_spectrum():
        for q in range(2):
            for p in range(SIDE // 2):
                for lanes in range(2):
                    wide[lanes, pl.ds((q * SIDE // 2 + p) * OWN, OWN), :] = near_taps[
                        q, :, pl.ds(p * SPAN + lanes * 128, 128)
                    ].astype(F32)
        lax.fori_loop(0, OWN // 4, near_filters, 0)

    def work():
        for lanes in range(2):
            wide[lanes, pl.ds(0, SIDE * OWN)] = (
                work_in[:, :, pl.ds(lanes * 128, 128)].astype(F32).reshape(SIDE * OWN, 128)
            )

        def four(i, carry):
            x = near_rows(i)
            f = near_spec[pl.ds(4 * i, 4)].reshape(4 * SIDE, 2 * SPAN)
            fr, fi = f[:, :SPAN], f[:, SPAN:]
            xr, xi = x[:, :SPAN], x[:, SPAN:]
            prod = jnp.concatenate([fr * xr - fi * xi, fr * xi + fi * xr], axis=1)
            mid = dot(prod.astype(BF16), inv[...])
            co, si = near_cos[...], near_sin[...]
            for n in range(2):
                parts = []
                for m in range(2):
                    top = (2 * n + m) * SIDE
                    re, im = mid[top : top + SIDE, :SPAN], mid[top : top + SIDE, SPAN:]
                    parts += [re * co - im * si, im * co + re * si]
                line = dot(near_last[...], jnp.concatenate(parts, axis=0).astype(BF16))
                for m in range(2):
                    for lanes in range(2):
                        back_wide[lanes, pl.ds(4 * i + 2 * n + m, SIDE, stride=OWN), :] = line[
                            m * SIDE : (m + 1) * SIDE, lanes * 128 : (lanes + 1) * 128
                        ]
            return carry

        lax.fori_loop(0, OWN // 4, four, 0)
        for lanes in range(2):
            work_b[:, :, pl.ds(lanes * 128, 128)] = (
                back_wide[lanes, pl.ds(0, SIDE * OWN)].astype(BF16).reshape(SIDE, OWN, 128)
            )

    def convolve(h, slot):
        for lanes in range(2):
            wide[lanes] = (
                recv_a[h, :, :, pl.ds(lanes * 128, 128)].astype(F32).reshape(PARTS * OWN, 128)
            )

        def channel_pair(i, carry):
            mids = []
            for n in range(2):
                c = 2 * i + n
                x = jnp.concatenate([column(wide, c), column(wide, HALF + c)], axis=0)
                mid = dot(pair[...], x.astype(BF16))
                mids += [twist(mid[: 2 * PARTS]), twist(mid[2 * PARTS :])]
            full = dot(jnp.concatenate(mids, axis=0), fwd[...])
            prods = []
            for n in range(2):
                f = spec[h * HALF + 2 * i + n]
                fr, fi = f[:, :SPAN], f[:, SPAN:]
                kv = full[2 * n * PARTS : (2 * n + 1) * PARTS]
                gg = full[(2 * n + 1) * PARTS : (2 * n + 2) * PARTS]
                kr, kj = kv[:, :SPAN], kv[:, SPAN:]
                gr, gj = gg[:, :SPAN], gg[:, SPAN:]
                prods += [
                    jnp.concatenate([fr * kr - fi * kj, fr * kj + fi * kr], axis=1),
                    jnp.concatenate([gr * fr + gj * fi, gj * fr - gr * fi], axis=1),
                    jnp.concatenate([gr * kr + gj * kj, gj * kr - gr * kj], axis=1),
                ]
            mid = dot(jnp.concatenate([q.astype(BF16) for q in prods], axis=0), inv[...])
            co, si = tcos[...], tsin[...]
            for n in range(2):
                c = 2 * i + n
                for a in range(3):
                    top = (3 * n + a) * PARTS
                    re, im = mid[top : top + PARTS, :SPAN], mid[top : top + PARTS, SPAN:]
                    y = jnp.concatenate([re * co - im * si, im * co + re * si], axis=0)
                    line = dot(last[...], y.astype(BF16))
                    for lanes in range(2):
                        piece = line[:, lanes * 128 : (lanes + 1) * 128]
                        if a < 2:
                            back_wide[lanes, pl.ds(a * HALF + c, PARTS, stride=OWN), :] = piece
                        else:
                            lag[slot, c // 4, lanes, pl.ds(c % 4, PARTS, stride=4), :] = piece
            return carry

        lax.fori_loop(0, HALF // 2, channel_pair, 0)
        here = pl.ds(pl.multiple_of(half * SIDE * OWN, OWN), SIDE * OWN)
        there = pl.ds(pl.multiple_of((1 - half) * SIDE * OWN, OWN), SIDE * OWN)
        chosen = []
        for lanes in range(2):
            send_b[h, :, :, pl.ds(lanes * 128, 128)] = (
                back_wide[lanes, here].astype(BF16).reshape(SIDE, OWN, 128)
            )
            pieces = back_wide[lanes, there].reshape(SIDE, 2, HALF, 128)
            chosen.append(jnp.where(half == 0, pieces[:, 0], pieces[:, 1]))
        send_c[h] = jnp.concatenate(chosen, axis=1).astype(BF16)

    def lag_swap(slot):
        return pltpu.make_async_remote_copy(
            src_ref=lag_out.at[slot],
            dst_ref=lag_in.at[slot],
            send_sem=ss_l.at[slot],
            recv_sem=rs_l.at[slot],
            device_id={"dp": other_core},
            device_id_type=MESH,
        )

    far = pltpu.make_async_remote_copy(
        src_ref=far_out,
        dst_ref=far_in,
        send_sem=ss_f.at[0],
        recv_sem=rs_f.at[0],
        device_id={"dp": other_cube},
        device_id_type=MESH,
    )

    for slot, h in enumerate(order):
        forward_whole(h).wait_recv()
        if slot == 1:
            lag_swap(0).wait_recv()
            far_out[...] = (lag[0, core] + lag_in[0].astype(F32)).astype(BF16)
            far.start()
        else:
            tap_copy(0).wait_recv()
            tap_copy(1).start()
        convolve(h, slot)
        send_planes(
            [
                (far_block(h), across), (return_block(h), beside),
                (far_block(h), behind), (return_block(h), z),
            ]
        )
        lag_out[slot] = lag[slot, 1 - core].astype(BF16)
        lag_swap(slot).start()
        if slot == 0:
            tap_copy(1).wait_recv()
            near_spectrum()
            work_whole.wait_recv()
            work()
            send_planes([(work_result, beside), (work_result, z)])

    lag_swap(1).wait_recv()
    far.wait_recv()
    for lanes in range(2):
        total = lag[1, core, lanes] + lag_in[1, lanes].astype(F32) + far_in[lanes].astype(F32)
        for p in range(PARTS):
            lag_sum[:, pl.ds(p * SPAN + lanes * 128, 128)] = total[4 * p : 4 * p + 4]
    lag_store = pltpu.make_async_copy(lag_sum, out_filter, kept.at[3])
    lag_store.start()

    for h in order:
        return_whole(h).wait_recv()
        far_whole(h).wait_recv()
    result_whole.wait_recv()

    for block in (return_block(0), return_block(1), work_result):
        src, dst, _, _, own = block(me)
        pltpu.make_async_copy(src, dst, own).wait()

    for h in order:
        forward_whole(h).wait_send()
        return_whole(h).wait_send()
        far_whole(h).wait_send()
    work_whole.wait_send()
    result_whole.wait_send()
    for step in range(2):
        tap_copy(step).wait_send()
    for slot in range(2):
        lag_swap(slot).wait_send()
    far.wait_send()
    lag_store.wait()


def finish(*refs):
    given, results, held, made = refs[:7], refs[7:11], refs[11:18], refs[18:21]
    loaded, stored = refs[21:]
    near, far, work, go, vi, ki, lags = held
    half = lax.axis_index("context") // SIDE

    def columns(side, n):
        plane = (half if side == 0 else 1 - half) * 2 + n
        return pl.ds(pl.multiple_of(plane * SPAN, SPAN), SPAN)

    def load(n, sem, view):
        return pltpu.make_async_copy(view(given[n]), view(held[n]), loaded.at[sem])

    steps, loads, sem = [(side, n) for side in range(2) for n in range(2)], [], 0
    for side, n in steps:
        part, cols = pl.ds(n * 16, 16), columns(side, n)
        block = lambda ref: ref.at[:, part]
        views = [(0, block)] if side == 0 else [(1, block), (2, lambda ref: ref.at[part])]
        views += [(m, lambda ref: ref.at[:, cols]) for m in (3, 4, 5)]
        group = []
        for m, view in views:
            group.append(load(m, sem, view))
            group[-1].start()
            sem += 1
        loads.append(group)
    passing = load(6, sem, lambda ref: ref)
    passing.start()

    def turn(rows):
        return rows.reshape(SPAN, SPAN).astype(F32).T

    stores = []
    for step, (side, n) in enumerate(steps):
        for one in loads[step]:
            one.wait()
        part, cols = pl.ds(n * 16, 16), columns(side, n)
        if side == 0:
            groups = [near[h, part].astype(F32) for h in range(2)]
            conv, back = [
                turn(jnp.concatenate([g[:, a * HALF : (a + 1) * HALF] for g in groups], axis=1))
                for a in range(2)
            ]
        else:
            pieces = [far[h, part].astype(F32) for h in range(2)]
            pieces = [jnp.concatenate([q[:, :HALF], q[:, HALF:]], axis=2) for q in pieces]
            owner, worker = turn(jnp.concatenate(pieces, axis=1)), turn(work[part])
            conv, back = jnp.where(half == 0, worker, owner), jnp.where(half == 0, owner, worker)
        for m, (left, right) in enumerate(((go, conv), (vi, back), (ki, back))):
            made[m][:, cols] = (left[:, cols].astype(F32) * right).astype(BF16)
            stores.append(
                pltpu.make_async_copy(
                    made[m].at[:, cols], results[m].at[:, cols], stored.at[3 * step + m]
                )
            )
            stores[-1].start()
        if step == 1:
            passing.wait()
            stores.append(pltpu.make_async_copy(lags, results[3], stored.at[12]))
            stores[-1].start()
    for one in stores:
        one.wait()


def on_device(grad_out, gate, key_in, value_in, filters):
    consts = [
        jnp.asarray(t.astype(np.float32) if n < 4 else np.asarray(t, dtype=jnp.bfloat16))
        for n, t in enumerate(tables())
    ]
    twists, (place, eye, *rest) = consts[:4], consts[4:]
    operands = (
        gate[0], key_in[0], value_in[0], grad_out[0], place, eye, filters, *twists, *rest,
    )
    dma = pltpu.SemaphoreType.DMA
    seq = jax.ShapeDtypeStruct((SPAN, 1024), BF16)
    lags = jax.ShapeDtypeStruct((4, LENGTH), F32)
    hbm = pl.BlockSpec(memory_space=pltpu.HBM)
    *blocks, grad_filter = pl.pallas_call(
        kernel,
        out_shape=(
            jax.ShapeDtypeStruct((2, SIDE, OWN, SPAN), BF16),
            jax.ShapeDtypeStruct((2, SIDE, OWN, 128), BF16),
            jax.ShapeDtypeStruct((SIDE, OWN, SPAN), BF16),
            lags,
        ),
        in_specs=[hbm] * OPERANDS,
        out_specs=(hbm,) * 4,
        scratch_shapes=[
            *[pltpu.VMEM(x.shape, x.dtype) for x in operands],
            dma((OPERANDS,)),
            pltpu.VMEM((4, SPAN, 2 * SPAN), BF16),
            pltpu.VMEM((2, PARTS, OWN, SPAN), BF16),
            pltpu.VMEM((2, PARTS, OWN, SPAN), BF16),
            pltpu.VMEM((2, SIDE, OWN, SPAN), BF16),
            pltpu.VMEM((2, SIDE, OWN, 128), BF16),
            *[pltpu.VMEM((SIDE, OWN, SPAN), BF16)] * 3,
            pltpu.VMEM((OWN, LENGTH // 4), BF16),
            pltpu.VMEM((2, OWN, LENGTH // 4), BF16),
            pltpu.VMEM((2, PARTS * OWN, 128), F32),
            pltpu.VMEM((2, PARTS * OWN, 128), F32),
            pltpu.VMEM((OWN, PARTS, 2 * SPAN), F32),
            pltpu.VMEM((OWN, SIDE, 2 * SPAN), F32),
            pltpu.VMEM((2, 2, 2, PARTS * 4, 128), F32),
            pltpu.VMEM((2, 2, PARTS * 4, 128), BF16),
            pltpu.VMEM((2, 2, PARTS * 4, 128), BF16),
            pltpu.VMEM((2, PARTS * 4, 128), BF16),
            pltpu.VMEM((2, PARTS * 4, 128), BF16),
            pltpu.VMEM((4, LENGTH), F32),
            *[dma((2,))] * 12, dma((1,)), dma((1,)), dma((4,)),
            pltpu.SemaphoreType.REGULAR,
        ],
        name="hyena_backward",
        compiler_params=pltpu.CompilerParams(
            collective_id=0, has_side_effects=True, vmem_limit_bytes=58 * 2**20
        ),
    )(*operands)
    operands = (*blocks, grad_out[0], value_in[0], key_in[0], grad_filter)
    grads = pl.pallas_call(
        finish,
        out_shape=(seq, seq, seq, lags),
        in_specs=[hbm] * 7,
        out_specs=(hbm,) * 4,
        scratch_shapes=[
            *[pltpu.VMEM(x.shape, x.dtype) for x in operands],
            *[pltpu.VMEM(seq.shape, seq.dtype)] * 3,
            dma((21,)),
            dma((13,)),
        ],
        name="products",
        compiler_params=pltpu.CompilerParams(vmem_limit_bytes=60 * 2**20),
    )(*operands)
    return (grads[0][None], grads[1][None], grads[2][None], grads[3])


def solution(mesh):
    return jax.shard_map(
        on_device,
        mesh=mesh,
        in_specs=(
            P("dp", "context", None),
            P("dp", "context", None),
            P("dp", "context", None),
            P("dp", "context", None),
            P("context", None),
        ),
        out_specs=(
            P("dp", "context", None),
            P("dp", "context", None),
            P("dp", "context", None),
            P(("context", "dp"), None),
        ),
        check_vma=False,
    )
```

```python
import functools

import jax
import jax.numpy as jnp
import numpy as np
from jax import lax
from jax.experimental import pallas as pl
from jax.experimental.pallas import tpu as pltpu
from jax.sharding import PartitionSpec as P

MESH = pl.DeviceIdType.MESH
F32 = jnp.float32
BF16 = jnp.bfloat16

SPAN = 256
PARTS = 64
OWN = 16
HALF = 8
LENGTH = SPAN * PARTS
SIDE = PARTS // 2
OPERANDS = 18


def tables():
    k1 = np.arange(PARTS)[:, None] + 0.25
    p = np.arange(PARTS)[None, :]
    angle = 2 * np.pi * k1 * p / PARTS
    first = np.concatenate([np.cos(angle), -np.sin(angle)], 0)
    zero = np.zeros_like(first)
    pair = np.block([[first, zero], [zero, first]])
    filt = np.concatenate([first, first], 1)
    last = np.concatenate([np.cos(angle).T, -np.sin(angle).T], 1) / LENGTH
    s = np.arange(SPAN)
    twist = 2 * np.pi * k1 * s[None, :] / LENGTH
    grid = 2 * np.pi * (s[:, None] * s[None, :] % SPAN) / SPAN
    cos, sin = np.cos(grid), np.sin(grid)
    forward = np.block([[cos, -sin], [sin, cos]])
    inverse = np.block([[cos, sin], [-sin, cos]])
    place = np.zeros((2, SPAN, 2 * SPAN))
    for h in range(2):
        for j in range(SPAN // OWN):
            for a in range(2):
                for c in range(HALF):
                    place[h, j * OWN + a * HALF + c, a * SPAN + j * OWN + h * HALF + c] = 1
    eye = np.eye(SPAN)
    k1 = np.arange(SIDE)[:, None] + 0.25
    angle = 2 * np.pi * k1 * np.arange(SIDE)[None, :] / SIDE
    first = np.concatenate([np.cos(angle), -np.sin(angle)], 0)
    near = np.block([[first, np.zeros_like(first)], [np.zeros_like(first), first]])
    final = np.concatenate([np.cos(angle).T, -np.sin(angle).T], 1) * 2 / LENGTH
    near_last = np.block([[final, np.zeros_like(final)], [np.zeros_like(final), final]])
    near_twist = 2 * np.pi * k1 * s[None, :] * 2 / LENGTH
    return (
        np.cos(twist), np.sin(twist), np.cos(near_twist), np.sin(near_twist),
        place, eye, filt, forward, near, pair, inverse, last, near_last,
    )


def dot(a, b):
    return jnp.dot(a, b, preferred_element_type=F32)


def dot_t(a, b):
    return lax.dot_general(a, b, (((1,), (1,)), ((), ())), preferred_element_type=F32)


def target(me, plane, k):
    x, y = (me // 4) % 4, me % 4
    return plane * 16 + ((x + k // 4) % 4) * 4 + (y + k % 4) % 4


def kernel(*refs):
    given, refs = refs[:OPERANDS], refs[OPERANDS:]
    results, refs = refs[:4], refs[4:]
    held, loaded, refs = refs[:OPERANDS], refs[OPERANDS], refs[OPERANDS + 1 :]
    loads = [
        pltpu.make_async_copy(src, dst, loaded.at[n])
        for n, (src, dst) in enumerate(zip(given, held))
    ]
    for load in loads:
        load.start()
    body(loads, *held, *results, *refs)


def body(
    loads,
    gt, ki, vi, go, place, eye, flt, tcos, tsin, near_cos, near_sin,
    filt, fwd, near, pair, inv, last, near_last,
    recv_b, recv_c, work_back, out_filter,
    both, send_a, recv_a, send_b, send_c, work_a, work_in, work_b,
    taps, near_taps, wide, back_wide, spec, near_spec, lag, lag_out, lag_in, far_out, far_in, lag_sum,
    ss_a, rs_a, ss_b, rs_b, ss_c, rs_c, ss_w, rs_w, ss_t, rs_t, ss_l, rs_l, ss_f, rs_f, kept, cross,
):
    dp, me = lax.axis_index("dp"), lax.axis_index("context")
    z_hi, core = dp // 2, dp % 2
    other_core = z_hi * 2 + (1 - core)
    other_cube = (1 - z_hi) * 2 + core

    barrier = pltpu.get_barrier_semaphore()

    z = me // 16
    half, odd = z // 2, z % 2
    across, behind = (1 - half) * 2 + odd, (1 - half) * 2 + (1 - odd)
    beside = half * 2 + (1 - odd)
    planes = (across, behind, beside, z)

    for plane in planes:

        def greet(k, carry, plane=plane):
            pl.semaphore_signal(
                barrier, inc=1, device_id={"context": target(me, plane, k)}, device_id_type=MESH
            )
            return carry

        lax.fori_loop(1 if plane is z else 0, 16, greet, 0)
    pl.semaphore_signal(barrier, inc=1, device_id={"dp": other_core}, device_id_type=MESH)
    twin = {"dp": other_cube, "context": (me + SIDE) % PARTS}
    partners = ({"dp": other_cube}, twin)

    for load in loads[:7]:
        load.wait()
    order = (1 - z_hi, z_hi)

    def rows_of(h, plane):
        rows = dot_t(place[h], both[plane]).astype(BF16)
        send_a[h, pl.ds(plane * 16, 16)] = rows.reshape(16, OWN, SPAN)

    mine = me % SIDE
    sums = pl.ds(0, PARTS * 4)

    def forward_block(h):
        return lambda d: (send_a.at[h, d], recv_a.at[h, me], ss_a.at[h], rs_a.at[h], None)

    def work_block(d):
        return work_a.at[d % SIDE], work_in.at[mine], ss_w.at[0], rs_w.at[0], None

    def return_block(h):
        return lambda d: (
            send_b.at[h, d % SIDE], recv_b.at[h, mine], ss_b.at[h], rs_b.at[h], kept.at[h],
        )

    def far_block(h):
        return lambda d: (send_c.at[h, d % SIDE], recv_c.at[h, mine], ss_c.at[h], rs_c.at[h], None)

    def work_result(d):
        return work_b.at[d % SIDE], work_back.at[mine], ss_w.at[1], rs_w.at[1], kept.at[2]

    def send(block, plane, k):
        d = target(me, plane, k)
        src, dst, ssem, rsem, _ = block(d)
        pltpu.make_async_remote_copy(
            src_ref=src,
            dst_ref=dst,
            send_sem=ssem,
            recv_sem=rsem,
            device_id={"context": d},
            device_id_type=MESH,
        ).start()

    def send_planes(jobs):
        def one(k, carry):
            for block, plane in jobs:
                send(block, plane, k)
            return carry

        lax.fori_loop(1, 16, one, 0)
        for block, plane in jobs:
            if plane is z:
                src, dst, _, _, own = block(me)
                if own is None:
                    dst[...] = src[...]
                else:
                    pltpu.make_async_copy(src, dst, own).start()
            else:
                send(block, plane, 0)

    def tap_copy(step):
        here = near_taps.at[core]
        return pltpu.make_async_remote_copy(
            src_ref=taps if step == 0 else here,
            dst_ref=here,
            send_sem=ss_t.at[step],
            recv_sem=rs_t.at[step],
            device_id=twin if step == 0 else {"dp": other_core},
            device_id_type=MESH,
        )

    first, second = order
    for n, plane in enumerate(planes):
        cols = pl.ds(pl.multiple_of(plane * SPAN, SPAN), SPAN)
        kv = (ki[:, cols].astype(F32) * vi[:, cols].astype(F32)).astype(BF16)
        gg = (go[:, cols].astype(F32) * gt[:, cols].astype(F32)).astype(BF16)
        both[plane] = jnp.concatenate([kv, gg], axis=1)
        rows_of(first, plane)
        if n == 0:
            taps[...] = flt[
                :, pl.ds(pl.multiple_of(core * (LENGTH // 4), LENGTH // 4), LENGTH // 4)
            ].astype(BF16)
            pl.semaphore_wait(barrier, PARTS + 2 * z_hi)

            @pl.when(z_hi == 0)
            def _():
                for partner in partners:
                    pl.semaphore_signal(barrier, inc=1, device_id=partner, device_id_type=MESH)

            @pl.when(z_hi == 1)
            def _():
                for partner in partners:
                    pl.semaphore_signal(cross, inc=1, device_id=partner, device_id_type=MESH)
                tap_copy(0).start()

            send_planes([(forward_block(first), plane)])
    send_planes([(forward_block(first), p) for p in (beside, behind, z)])

    @pl.when(z_hi == 0)
    def _():
        pl.semaphore_wait(cross, 2)
        tap_copy(0).start()

    rows_of(second, across)
    rows_of(second, behind)
    for n in range(2):
        one_array = both[(1 - half) * 2 + n, :, pl.ds(pl.multiple_of(half * SPAN, SPAN), SPAN)]
        work_a[pl.ds(n * 16, 16)] = dot_t(eye[...], one_array).astype(BF16).reshape(16, OWN, SPAN)
    send_planes(
        [
            (forward_block(second), across), (work_block, beside),
            (forward_block(second), behind), (work_block, z),
        ]
    )
    rows_of(second, beside)
    rows_of(second, z)
    send_planes([(forward_block(second), beside), (forward_block(second), z)])

    def whole(src, dst, count, ssem, rsem):
        return pltpu.make_async_remote_copy(
            src_ref=src.at[pl.ds(0, count)],
            dst_ref=dst.at[pl.ds(0, count)],
            send_sem=ssem,
            recv_sem=rsem,
            device_id={"context": me},
            device_id_type=MESH,
        )

    def forward_whole(h):
        return whole(send_a.at[h], recv_a.at[h], PARTS - 1, ss_a.at[h], rs_a.at[h])

    def return_whole(h):
        return whole(send_b.at[h], recv_b.at[h], SIDE - 1, ss_b.at[h], rs_b.at[h])

    def far_whole(h):
        return whole(send_c.at[h], recv_c.at[h], SIDE, ss_c.at[h], rs_c.at[h])

    work_whole = whole(work_a, work_in, SIDE - 1, ss_w.at[0], rs_w.at[0])
    result_whole = whole(work_b, work_back, SIDE - 1, ss_w.at[1], rs_w.at[1])

    for load in loads[7:]:
        load.wait()

    def lay(p, carry):
        cols = pl.ds(pl.multiple_of(p * SPAN, SPAN), SPAN)
        for lanes in range(2):
            wide[lanes, pl.ds(pl.multiple_of(p * OWN, OWN), OWN), :] = flt[
                :, pl.ds(pl.multiple_of(p * SPAN + lanes * 128, 128), 128)
            ]
        return carry

    lax.fori_loop(0, PARTS, lay, 0)

    def column(ref, row, parts=PARTS):
        return jnp.concatenate(
            [ref[lanes, pl.ds(row, parts, stride=OWN), :] for lanes in range(2)], axis=1
        )

    def twist(mid, cos=tcos, sin=tsin):
        parts = cos.shape[0]
        re, im = mid[:parts], mid[parts:]
        c, s = cos[...], sin[...]
        return jnp.concatenate([re * c + im * s, im * c - re * s], axis=1).astype(BF16)

    def filter_pair(i, carry):
        mids = []
        for n in range(2):
            x = column(wide, 2 * i + n)
            high = x.astype(BF16)
            low = (x - high.astype(F32)).astype(BF16)
            mids.append(twist(dot(filt[...], jnp.concatenate([high, low], axis=0))))
        full = dot(jnp.concatenate(mids, axis=0), fwd[...])
        spec[pl.ds(2 * i, 2)] = full.reshape(2, PARTS, 2 * SPAN)
        return carry

    lax.fori_loop(0, OWN // 2, filter_pair, 0)

    def near_rows(i):
        mids = []
        for n in range(2):
            x = [column(wide, 4 * i + 2 * n + m, SIDE) for m in range(2)]
            mid = dot(near[...], jnp.concatenate(x, axis=0).astype(BF16))
            for m in range(2):
                mids.append(twist(mid[2 * m * SIDE : 2 * (m + 1) * SIDE], near_cos, near_sin))
        return dot(jnp.concatenate(mids, axis=0), fwd[...])

    def near_filters(i, carry):
        full = near_rows(i)
        im = jnp.where(half == 0, full[:, SPAN:], -full[:, SPAN:])
        full = jnp.concatenate([full[:, :SPAN], im], axis=1)
        near_spec[pl.ds(4 * i, 4)] = full.reshape(4, SIDE, 2 * SPAN)
        return carry

    def near_spectrum():
        for q in range(2):
            for p in range(SIDE // 2):
                for lanes in range(2):
                    wide[lanes, pl.ds((q * SIDE // 2 + p) * OWN, OWN), :] = near_taps[
                        q, :, pl.ds(p * SPAN + lanes * 128, 128)
                    ].astype(F32)
        lax.fori_loop(0, OWN // 4, near_filters, 0)

    def work():
        for lanes in range(2):
            wide[lanes, pl.ds(0, SIDE * OWN)] = (
                work_in[:, :, pl.ds(lanes * 128, 128)].astype(F32).reshape(SIDE * OWN, 128)
            )

        def four(i, carry):
            x = near_rows(i)
            f = near_spec[pl.ds(4 * i, 4)].reshape(4 * SIDE, 2 * SPAN)
            fr, fi = f[:, :SPAN], f[:, SPAN:]
            xr, xi = x[:, :SPAN], x[:, SPAN:]
            prod = jnp.concatenate([fr * xr - fi * xi, fr * xi + fi * xr], axis=1)
            mid = dot(prod.astype(BF16), inv[...])
            co, si = near_cos[...], near_sin[...]
            for n in range(2):
                parts = []
                for m in range(2):
                    top = (2 * n + m) * SIDE
                    re, im = mid[top : top + SIDE, :SPAN], mid[top : top + SIDE, SPAN:]
                    parts += [re * co - im * si, im * co + re * si]
                line = dot(near_last[...], jnp.concatenate(parts, axis=0).astype(BF16))
                for m in range(2):
                    for lanes in range(2):
                        back_wide[lanes, pl.ds(4 * i + 2 * n + m, SIDE, stride=OWN), :] = line[
                            m * SIDE : (m + 1) * SIDE, lanes * 128 : (lanes + 1) * 128
                        ]
            return carry

        lax.fori_loop(0, OWN // 4, four, 0)
        for lanes in range(2):
            work_b[:, :, pl.ds(lanes * 128, 128)] = (
                back_wide[lanes, pl.ds(0, SIDE * OWN)].astype(BF16).reshape(SIDE, OWN, 128)
            )

    def convolve(h, slot):
        for lanes in range(2):
            wide[lanes, pl.ds(0, PARTS * OWN)] = (
                recv_a[h, :, :, pl.ds(lanes * 128, 128)].astype(F32).reshape(PARTS * OWN, 128)
            )

        def channel_pair(i, carry):
            mids = []
            for n in range(2):
                c = 2 * i + n
                x = jnp.concatenate([column(wide, c), column(wide, HALF + c)], axis=0)
                mid = dot(pair[...], x.astype(BF16))
                mids += [twist(mid[: 2 * PARTS]), twist(mid[2 * PARTS :])]
            full = dot(jnp.concatenate(mids, axis=0), fwd[...])
            prods = []
            for n in range(2):
                f = spec[h * HALF + 2 * i + n]
                fr, fi = f[:, :SPAN], f[:, SPAN:]
                kv = full[2 * n * PARTS : (2 * n + 1) * PARTS]
                gg = full[(2 * n + 1) * PARTS : (2 * n + 2) * PARTS]
                kr, kj = kv[:, :SPAN], kv[:, SPAN:]
                gr, gj = gg[:, :SPAN], gg[:, SPAN:]
                prods += [
                    jnp.concatenate([fr * kr - fi * kj, fr * kj + fi * kr], axis=1),
                    jnp.concatenate([gr * fr + gj * fi, gj * fr - gr * fi], axis=1),
                    jnp.concatenate([gr * kr + gj * kj, gj * kr - gr * kj], axis=1),
                ]
            mid = dot(jnp.concatenate([q.astype(BF16) for q in prods], axis=0), inv[...])
            co, si = tcos[...], tsin[...]
            for n in range(2):
                c = 2 * i + n
                for a in range(3):
                    top = (3 * n + a) * PARTS
                    re, im = mid[top : top + PARTS, :SPAN], mid[top : top + PARTS, SPAN:]
                    y = jnp.concatenate([re * co - im * si, im * co + re * si], axis=0)
                    line = dot(last[...], y.astype(BF16))
                    for lanes in range(2):
                        piece = line[:, lanes * 128 : (lanes + 1) * 128]
                        if a < 2:
                            back_wide[lanes, pl.ds(a * HALF + c, PARTS, stride=OWN), :] = piece
                        else:
                            lag[slot, c // 4, lanes, pl.ds(c % 4, PARTS, stride=4), :] = piece
            return carry

        lax.fori_loop(0, HALF // 2, channel_pair, 0)
        here = pl.ds(pl.multiple_of(half * SIDE * OWN, OWN), SIDE * OWN)
        there = pl.ds(pl.multiple_of((1 - half) * SIDE * OWN, OWN), SIDE * OWN)
        chosen = []
        for lanes in range(2):
            send_b[h, :, :, pl.ds(lanes * 128, 128)] = (
                back_wide[lanes, here].astype(BF16).reshape(SIDE, OWN, 128)
            )
            pieces = back_wide[lanes, there].reshape(SIDE, 2, HALF, 128)
            chosen.append(jnp.where(half == 0, pieces[:, 0], pieces[:, 1]))
        send_c[h] = jnp.concatenate(chosen, axis=1).astype(BF16)

    def lag_swap(slot):
        return pltpu.make_async_remote_copy(
            src_ref=lag_out.at[slot],
            dst_ref=lag_in.at[slot],
            send_sem=ss_l.at[slot],
            recv_sem=rs_l.at[slot],
            device_id={"dp": other_core},
            device_id_type=MESH,
        )

    far = pltpu.make_async_remote_copy(
        src_ref=far_out,
        dst_ref=far_in,
        send_sem=ss_f.at[0],
        recv_sem=rs_f.at[0],
        device_id={"dp": other_cube},
        device_id_type=MESH,
    )

    for slot, h in enumerate(order):
        forward_whole(h).wait_recv()
        if slot == 1:
            lag_swap(0).wait_recv()
            far_out[...] = (lag[0, core, :, sums] + lag_in[0].astype(F32)).astype(BF16)
            far.start()
        else:
            tap_copy(0).wait_recv()
            tap_copy(1).start()
        convolve(h, slot)
        send_planes(
            [
                (far_block(h), across), (return_block(h), beside),
                (far_block(h), behind), (return_block(h), z),
            ]
        )
        lag_out[slot] = lag[slot, 1 - core, :, sums].astype(BF16)
        lag_swap(slot).start()
        if slot == 0:
            tap_copy(1).wait_recv()
            near_spectrum()
            work_whole.wait_recv()
            work()
            send_planes([(work_result, beside), (work_result, z)])

    lag_swap(1).wait_recv()
    far.wait_recv()
    for lanes in range(2):
        total = lag[1, core, lanes, sums] + lag_in[1, lanes].astype(F32) + far_in[lanes].astype(F32)
        for p in range(PARTS):
            lag_sum[:, pl.ds(p * SPAN + lanes * 128, 128)] = total[4 * p : 4 * p + 4]
    lag_store = pltpu.make_async_copy(lag_sum, out_filter, kept.at[3])
    lag_store.start()

    for h in order:
        return_whole(h).wait_recv()
        far_whole(h).wait_recv()
    result_whole.wait_recv()

    for block in (return_block(0), return_block(1), work_result):
        src, dst, _, _, own = block(me)
        pltpu.make_async_copy(src, dst, own).wait()

    for h in order:
        forward_whole(h).wait_send()
        return_whole(h).wait_send()
        far_whole(h).wait_send()
    work_whole.wait_send()
    result_whole.wait_send()
    for step in range(2):
        tap_copy(step).wait_send()
    for slot in range(2):
        lag_swap(slot).wait_send()
    far.wait_send()
    lag_store.wait()


def finish(*refs):
    given, results, held, made = refs[:7], refs[7:11], refs[11:18], refs[18:21]
    loaded, stored = refs[21:]
    near, far, work, go, vi, ki, lags = held
    half = lax.axis_index("context") // SIDE

    def columns(side, n):
        plane = (half if side == 0 else 1 - half) * 2 + n
        return pl.ds(pl.multiple_of(plane * SPAN, SPAN), SPAN)

    def load(n, sem, view):
        return pltpu.make_async_copy(view(given[n]), view(held[n]), loaded.at[sem])

    steps, loads, sem = [(side, n) for side in range(2) for n in range(2)], [], 0
    for side, n in steps:
        part, cols = pl.ds(n * 16, 16), columns(side, n)
        block = lambda ref: ref.at[:, part]
        views = [(0, block)] if side == 0 else [(1, block), (2, lambda ref: ref.at[part])]
        views += [(m, lambda ref: ref.at[:, cols]) for m in (3, 4, 5)]
        group = []
        for m, view in views:
            group.append(load(m, sem, view))
            group[-1].start()
            sem += 1
        loads.append(group)
    passing = load(6, sem, lambda ref: ref)
    passing.start()

    def turn(rows):
        return rows.reshape(SPAN, SPAN).astype(F32).T

    stores = []
    for step, (side, n) in enumerate(steps):
        for one in loads[step]:
            one.wait()
        part, cols = pl.ds(n * 16, 16), columns(side, n)
        if side == 0:
            groups = [near[h, part].astype(F32) for h in range(2)]
            conv, back = [
                turn(jnp.concatenate([g[:, a * HALF : (a + 1) * HALF] for g in groups], axis=1))
                for a in range(2)
            ]
        else:
            pieces = [far[h, part].astype(F32) for h in range(2)]
            pieces = [jnp.concatenate([q[:, :HALF], q[:, HALF:]], axis=2) for q in pieces]
            owner, worker = turn(jnp.concatenate(pieces, axis=1)), turn(work[part])
            conv, back = jnp.where(half == 0, worker, owner), jnp.where(half == 0, owner, worker)
        for m, (left, right) in enumerate(((go, conv), (vi, back), (ki, back))):
            made[m][:, cols] = (left[:, cols].astype(F32) * right).astype(BF16)
            stores.append(
                pltpu.make_async_copy(
                    made[m].at[:, cols], results[m].at[:, cols], stored.at[3 * step + m]
                )
            )
            stores[-1].start()
        if step == 1:
            passing.wait()
            stores.append(pltpu.make_async_copy(lags, results[3], stored.at[12]))
            stores[-1].start()
    for one in stores:
        one.wait()


def on_device(grad_out, gate, key_in, value_in, filters):
    consts = [
        jnp.asarray(t.astype(np.float32) if n < 4 else np.asarray(t, dtype=jnp.bfloat16))
        for n, t in enumerate(tables())
    ]
    twists, (place, eye, *rest) = consts[:4], consts[4:]
    operands = (
        gate[0], key_in[0], value_in[0], grad_out[0], place, eye, filters, *twists, *rest,
    )
    dma = pltpu.SemaphoreType.DMA
    seq = jax.ShapeDtypeStruct((SPAN, 1024), BF16)
    lags = jax.ShapeDtypeStruct((4, LENGTH), F32)
    hbm = pl.BlockSpec(memory_space=pltpu.HBM)
    *blocks, grad_filter = pl.pallas_call(
        kernel,
        out_shape=(
            jax.ShapeDtypeStruct((2, SIDE, OWN, SPAN), BF16),
            jax.ShapeDtypeStruct((2, SIDE, OWN, 128), BF16),
            jax.ShapeDtypeStruct((SIDE, OWN, SPAN), BF16),
            lags,
        ),
        in_specs=[hbm] * OPERANDS,
        out_specs=(hbm,) * 4,
        scratch_shapes=[
            *[pltpu.VMEM(x.shape, x.dtype) for x in operands],
            dma((OPERANDS,)),
            pltpu.VMEM((4, SPAN, 2 * SPAN), BF16),
            pltpu.VMEM((2, PARTS, OWN, SPAN), BF16),
            pltpu.VMEM((2, PARTS, OWN, SPAN), BF16),
            pltpu.VMEM((2, SIDE, OWN, SPAN), BF16),
            pltpu.VMEM((2, SIDE, OWN, 128), BF16),
            *[pltpu.VMEM((SIDE, OWN, SPAN), BF16)] * 3,
            pltpu.VMEM((OWN, LENGTH // 4), BF16),
            pltpu.VMEM((2, OWN, LENGTH // 4), BF16),
            pltpu.VMEM((2, (PARTS + 1) * OWN, 128), F32),
            pltpu.VMEM((2, (PARTS + 1) * OWN, 128), F32),
            pltpu.VMEM((OWN, PARTS, 2 * SPAN), F32),
            pltpu.VMEM((OWN, SIDE, 2 * SPAN), F32),
            pltpu.VMEM((2, 2, 2, PARTS * 4 + 8, 128), F32),
            pltpu.VMEM((2, 2, PARTS * 4, 128), BF16),
            pltpu.VMEM((2, 2, PARTS * 4, 128), BF16),
            pltpu.VMEM((2, PARTS * 4, 128), BF16),
            pltpu.VMEM((2, PARTS * 4, 128), BF16),
            pltpu.VMEM((4, LENGTH), F32),
            *[dma((2,))] * 12, dma((1,)), dma((1,)), dma((4,)),
            pltpu.SemaphoreType.REGULAR,
        ],
        name="hyena_backward",
        compiler_params=pltpu.CompilerParams(
            collective_id=0, has_side_effects=True, vmem_limit_bytes=58 * 2**20
        ),
    )(*operands)
    operands = (*blocks, grad_out[0], value_in[0], key_in[0], grad_filter)
    grads = pl.pallas_call(
        finish,
        out_shape=(seq, seq, seq, lags),
        in_specs=[hbm] * 7,
        out_specs=(hbm,) * 4,
        scratch_shapes=[
            *[pltpu.VMEM(x.shape, x.dtype) for x in operands],
            *[pltpu.VMEM(seq.shape, seq.dtype)] * 3,
            dma((21,)),
            dma((13,)),
        ],
        name="products",
        compiler_params=pltpu.CompilerParams(vmem_limit_bytes=60 * 2**20),
    )(*operands)
    return (grads[0][None], grads[1][None], grads[2][None], grads[3])


def solution(mesh):
    return jax.shard_map(
        on_device,
        mesh=mesh,
        in_specs=(
            P("dp", "context", None),
            P("dp", "context", None),
            P("dp", "context", None),
            P("dp", "context", None),
            P("context", None),
        ),
        out_specs=(
            P("dp", "context", None),
            P("dp", "context", None),
            P("dp", "context", None),
            P(("context", "dp"), None),
        ),
        check_vma=False,
    )
```
